256 devices in a mesh: group: 4 (over y), dev: 64 (over z, x, core).
Axes of the slice: x: 4, y: 4, z: 8, core: 2. Of those that a mesh axis runs over, the one named last changes fastest.
Arguments:
- tokens: bfloat16 [256, 512, 1024], P(('group', 'dev')), may hold values from -12 to 12
- pair_list: int32 [256, 2], P(('group', 'dev')), may hold values from 0 to 255, as said below
- confidence: int32 [256, 2, 512], P(('group', 'dev')), may hold values from 1 to 32
- w_embed: bfloat16 [1024, 768], replicated, may hold values from -0.1875 to 0.1875
- w_query: bfloat16 [768, 768], replicated, may hold values from -0.21875 to 0.21875
- w_key: bfloat16 [768, 768], replicated, may hold values from -0.21875 to 0.21875
- w_value: bfloat16 [768, 768], replicated, may hold values from -0.21875 to 0.21875
- w_out: bfloat16 [768, 768], replicated, may hold values from -0.21875 to 0.21875
- norm_gain: float32 [768], replicated, may hold values from 0.25 to 1.75
- w_head: bfloat16 [768, 3456], replicated, may hold values from -0.21875 to 0.21875
Outputs:
- merged_maps: bfloat16 [256, 512, 3456], P(('group', 'dev'))
The draws below stay inside these ranges and needn't reach their ends.
Inputs may be any that keep to these rules, and one draw needn't show every extreme that they name: `pair_list`: each pair names two different images whose indices differ from the pair's own index by at most one.
All inputs are finite; a program needn't handle non-finite values.
Results may differ from the reference program's by a relative error of at most 0.012.
Values may be sent and summed in bfloat16 or wider, within the bound.
A program may use at most 128 MiB of HBM per device.

```python
import jax
import jax.numpy as jnp
from jax import lax

DIN = 1024
DM = 768
HEADS = 12
HEAD_DIM = 64
HEAD_OUT = 3456
TOK = 512
IMAGES = 256
PAIRS = 256


def draw_tokens(key, part):
    key = jax.random.fold_in(key, 11)
    base_key = jax.random.fold_in(key, 0)
    values = jnp.clip(jax.random.normal(base_key, (IMAGES, TOK, DIN), jnp.float32), -6.0, 6.0)
    return values.astype(jnp.bfloat16)


def draw_pair_list(key, part):
    key = jax.random.fold_in(key, 23)
    flip = jax.random.randint(key, (PAIRS,), 0, 2)
    index = jnp.arange(PAIRS, dtype=jnp.int32)
    low = jnp.where(index == 0, 0, index - 1)
    high = jnp.where(index == PAIRS - 1, PAIRS - 1, index + 1)
    first = jnp.where(flip == 1, high, low)
    second = jnp.where(flip == 1, low, high)
    return jnp.stack([first, second], axis=1).astype(jnp.int32)


def plant(result, rng, low, top_value):
    dims = result.shape
    place = [jax.random.randint(jax.random.fold_in(rng, axis), (), 0, dims[axis]) for axis in range(len(dims))]
    result = result.at[tuple(place)].set(low)
    longest = dims.index(max(dims))
    place[longest] = (place[longest] + 1) % dims[longest]
    return result.at[tuple(place)].set(top_value)


def normal_values(stream_key, dims, scale, limit, held_as=jnp.bfloat16):
    drawn = jax.random.normal(stream_key, dims, jnp.float32) * scale
    return jnp.minimum(jnp.maximum(drawn, -limit), limit).astype(held_as)


def setup_inputs(seed: int = 0) -> dict:
    key_of = jax.random.split(jax.random.key(seed), 11)
    tokens = draw_tokens(jax.random.fold_in(key_of[10], 71), 0)
    pair_list = draw_pair_list(jax.random.fold_in(key_of[10], 71), 0)
    confidence = plant(jax.random.randint(key_of[2], (PAIRS, 2, TOK), 1, 33), jax.random.fold_in(key_of[2], 1), 1, 32).astype(jnp.int32)
    w_embed = normal_values(key_of[3], (DIN, DM), DIN ** -0.5, 0.1875)
    w_query = normal_values(key_of[4], (DM, DM), DM ** -0.5, 0.21875)
    w_key = normal_values(key_of[5], (DM, DM), DM ** -0.5, 0.21875)
    w_value = normal_values(key_of[6], (DM, DM), DM ** -0.5, 0.21875)
    w_out = normal_values(key_of[7], (DM, DM), DM ** -0.5, 0.21875)
    norm_gain = jnp.clip(1.0 + 0.15 * jax.random.normal(key_of[8], (DM,), jnp.float32), 0.25, 1.75)
    w_head = normal_values(key_of[9], (DM, HEAD_OUT), DM ** -0.5, 0.21875)
    return dict(tokens=tokens, pair_list=pair_list, confidence=confidence, w_embed=w_embed, w_query=w_query, w_key=w_key, w_value=w_value, w_out=w_out, norm_gain=norm_gain, w_head=w_head)


def cross_branch(x_q, x_kv, w_query, w_key, w_value, w_out, norm_gain, w_head):
    tok = x_q.shape[0]
    q = jnp.dot(x_q, w_query, preferred_element_type=jnp.float32).astype(jnp.bfloat16)
    k = jnp.dot(x_kv, w_key, preferred_element_type=jnp.float32).astype(jnp.bfloat16)
    v = jnp.dot(x_kv, w_value, preferred_element_type=jnp.float32).astype(jnp.bfloat16)

    def split(m):
        return m.reshape(tok, HEADS // 4, 4, HEAD_DIM).transpose(1, 2, 0, 3)

    def attend(blocks):
        qb, kb, vb = blocks
        scores = jnp.einsum('htd,hsd->hts', qb.astype(jnp.float32), kb.astype(jnp.float32)) / HEAD_DIM ** 0.5
        top = lax.optimization_barrier(jnp.max(scores, axis=-1, keepdims=True))
        expo = jnp.exp(scores - top)
        probs = (expo / lax.optimization_barrier(jnp.sum(expo, axis=-1, keepdims=True))).astype(jnp.bfloat16)
        return jnp.einsum('hts,hsd->htd', probs.astype(jnp.float32), vb.astype(jnp.float32))
    ctx = lax.map(attend, (split(q), split(k), split(v)))
    context = ctx.transpose(2, 0, 1, 3).reshape(tok, HEADS * HEAD_DIM).astype(jnp.bfloat16)
    mixed = x_q.astype(jnp.float32) + jnp.dot(context, w_out, preferred_element_type=jnp.float32)
    center = mixed - lax.optimization_barrier(jnp.mean(mixed, axis=-1, keepdims=True))
    spread = lax.optimization_barrier(jnp.mean(center * center, axis=-1, keepdims=True))
    normed = (center / jnp.sqrt(spread + 1e-06) * norm_gain).astype(jnp.bfloat16)
    return jnp.dot(normed, w_head, preferred_element_type=jnp.float32)

def reference(tokens, pair_list, confidence, w_embed, w_query, w_key, w_value, w_out, norm_gain, w_head):
    embedded = lax.map(lambda t: jnp.dot(t, w_embed, preferred_element_type=jnp.float32).astype(jnp.bfloat16), tokens)
    count = tokens.shape[0]
    total0 = jnp.zeros((count, tokens.shape[1], w_head.shape[1]), jnp.float32)
    weight0 = jnp.zeros((count, tokens.shape[1]), jnp.float32)

    def one_pair(carry, item):
        total, weight = carry
        pair, conf = item
        first = embedded[pair[0]]
        second = embedded[pair[1]]
        out_a = cross_branch(first, second, w_query, w_key, w_value, w_out, norm_gain, w_head)
        out_b = cross_branch(second, first, w_query, w_key, w_value, w_out, norm_gain, w_head)
        conf_a = conf[0].astype(jnp.float32)
        conf_b = conf[1].astype(jnp.float32)
        total = total.at[pair[0]].add(conf_a[:, None] * out_a)
        total = total.at[pair[1]].add(conf_b[:, None] * out_b)
        weight = weight.at[pair[0]].add(conf_a)
        weight = weight.at[pair[1]].add(conf_b)
        return ((total, weight), jnp.zeros((), jnp.float32))
    (total, weight), unused = lax.scan(one_pair, (total0, weight0), (pair_list, confidence))
    return (total / jnp.maximum(weight, 1.0)[:, :, None]).astype(jnp.bfloat16)
```

```python
import functools

import jax
import jax.numpy as jnp
from jax import lax
from jax.experimental import pallas as pl
from jax.experimental.pallas import tpu as pltpu
from jax.sharding import PartitionSpec as P

HEADS = 12
HEAD_DIM = 64
PAIRED = 2 * HEAD_DIM
LOG2E = 1.4426950408889634
MESH = pl.DeviceIdType.MESH
BF16 = jnp.bfloat16
F32 = jnp.float32
SEND_ROWS = 128
ROWS = 128


def dot(a, b):
    return jnp.dot(a, b, preferred_element_type=F32)


def kernel(
    mesh_shape,
    pair_ref,
    conf_ref,
    gain_ref,
    tokens_hbm,
    w_embed_hbm,
    w_query_hbm,
    w_key_hbm,
    w_value_hbm,
    w_out_hbm,
    merged_ref,
    tokens,
    w_embed,
    w_query,
    w_key,
    w_value,
    w_out,
    own,
    from_fast,
    from_slow,
    x_u,
    q_even,
    q_odd,
    k_u,
    k_w,
    v_even_u,
    v_odd_u,
    v_even_w,
    v_odd_w,
    context,
    normed_u,
    normed_w,
    back_fast,
    back_slow,
    conf_out,
    conf_fast,
    conf_slow,
    load_sem,
    send_sem,
    recv_fast_sem,
    recv_slow_sem,
    send_back_sem,
    recv_back_fast_sem,
    recv_back_slow_sem,
    conf_sem,
):
    n_group, n_dev = mesh_shape
    n = n_group * n_dev
    me = lax.axis_index("group") * n_dev + lax.axis_index("dev")
    odd = lax.rem(me, 2)
    fast = me + 1 - 2 * odd
    slow = lax.rem(me + 2 * odd - 1 + n, n)
    fast_id = (lax.div(fast, n_dev), lax.rem(fast, n_dev))
    slow_id = (lax.div(slow, n_dev), lax.rem(slow, n_dev))

    loads = [
        pltpu.make_async_copy(src, dst, load_sem.at[i])
        for i, (src, dst) in enumerate(
            (
                (tokens_hbm, tokens),
                (w_embed_hbm, w_embed),
                (w_key_hbm, w_key),
                (w_value_hbm, w_value),
                (w_query_hbm, w_query),
                (w_out_hbm, w_out),
            )
        )
    ]
    for load in loads:
        load.start()

    barrier = pltpu.get_barrier_semaphore()
    pl.semaphore_signal(barrier, inc=1, device_id=fast_id, device_id_type=MESH)
    pl.semaphore_signal(barrier, inc=1, device_id=slow_id, device_id_type=MESH)

    first, second = pair_ref[0, 0], pair_ref[0, 1]
    has_fast = jnp.logical_or(first == fast, second == fast)
    has_slow = jnp.logical_or(first == slow, second == slow)
    u_image = jnp.where(has_fast, fast, me)
    u_first = (first == u_image).astype(F32)
    f_fast, f_slow = has_fast.astype(F32), has_slow.astype(F32)
    conf_first = conf_ref[0, 0:1, :].astype(F32)
    conf_second = conf_ref[0, 1:2, :].astype(F32)
    conf_u = conf_first * u_first + conf_second * (1.0 - u_first)
    conf_w = conf_second * u_first + conf_first * (1.0 - u_first)
    conf_out[...] = jnp.concatenate(
        [
            conf_u * f_fast,
            conf_w * f_slow,
            conf_u * (1.0 - f_fast),
            conf_w * (1.0 - f_slow),
            jnp.zeros((4, conf_u.shape[1]), F32),
        ],
        axis=0,
    )
    pl.semaphore_wait(barrier, 2)

    def remote(src, dst, send, recv, target):
        return pltpu.make_async_remote_copy(
            src_ref=src,
            dst_ref=dst,
            send_sem=send,
            recv_sem=recv,
            device_id=target,
            device_id_type=MESH,
        )

    def rows_of(step, size):
        return pl.ds(pl.multiple_of(step * size, size), size)

    tok = own.shape[0]
    sends = tok // SEND_ROWS
    steps = tok // ROWS

    def to_fast(i):
        block = rows_of(i, SEND_ROWS)
        return remote(own.at[block], from_fast.at[block], send_sem.at[0, i], recv_fast_sem.at[i], fast_id)

    def to_slow(i):
        block = rows_of(i, SEND_ROWS)
        return remote(own.at[block], from_slow.at[block], send_sem.at[1, i], recv_slow_sem.at[i], slow_id)

    def conf_copies():
        return (
            remote(conf_out, conf_fast, conf_sem.at[0], conf_sem.at[1], fast_id),
            remote(conf_out, conf_slow, conf_sem.at[2], conf_sem.at[3], slow_id),
        )

    loads[0].wait()
    loads[1].wait()

    def embed(i, carry):
        block = rows_of(i, SEND_ROWS)
        own[block, :] = dot(tokens[0, block, :], w_embed[...]).astype(BF16)
        to_slow(i).start()
        to_fast(i).start()
        return carry

    lax.fori_loop(0, sends, embed, 0)
    for copy in conf_copies():
        copy.start()

    lower_half = lax.broadcasted_iota(jnp.int32, (1, HEADS * HEAD_DIM), 1) % PAIRED < HEAD_DIM

    def put_query(block, x):
        q = dot(x, w_query[...]) * (LOG2E / HEAD_DIM**0.5)
        q_even[block, :] = jnp.where(lower_half, q, 0.0).astype(BF16)
        q_odd[block, :] = jnp.where(lower_half, 0.0, q).astype(BF16)

    def put_key_value(block, x, k_ref, v_even_ref, v_odd_ref):
        k_ref[block, :] = dot(x, w_key[...]).astype(BF16)
        v = dot(x, w_value[...])
        v_even_ref[block, :] = jnp.where(lower_half, v, 1.0).astype(BF16)
        v_odd_ref[block, :] = jnp.where(lower_half, 1.0, v).astype(BF16)

    half = lax.broadcasted_iota(jnp.int32, (1, PAIRED), 1) < HEAD_DIM

    def attend(block, x, k_ref, v_even_ref, v_odd_ref):
        for j in range(HEADS // 2):
            lanes = slice(j * PAIRED, (j + 1) * PAIRED)
            k = k_ref[:, lanes]
            both = []
            for q_ref, v_ref in ((q_even, v_even_ref), (q_odd, v_odd_ref)):
                scores = lax.dot_general(
                    q_ref[block, lanes], k, (((1,), (1,)), ((), ())), preferred_element_type=F32
                )
                top = jnp.max(scores, axis=1, keepdims=True)
                expo = jnp.exp2(scores - top).astype(BF16)
                both.append(dot(expo, v_ref[:, lanes]))
            even, odd_ = both
            total = jnp.where(half, even, odd_)
            weight = pltpu.roll(jnp.where(half, odd_, even), HEAD_DIM, 1)
            context[block, lanes] = (total / weight).astype(BF16)
        mixed = x.astype(F32) + dot(context[block, :], w_out[...])
        center = mixed - jnp.mean(mixed, axis=-1, keepdims=True)
        spread = jnp.mean(center * center, axis=-1, keepdims=True)
        return (center * lax.rsqrt(spread + 1e-06) * gain_ref[...]).astype(BF16)

    for load in loads[2:]:
        load.wait()

    def take_u(i, carry):
        to_fast(i).wait_recv()
        block = rows_of(i, SEND_ROWS)
        x = jnp.where(has_fast, from_fast[block, :], own[block, :])
        x_u[block, :] = x
        put_key_value(block, x, k_u, v_even_u, v_odd_u)
        return carry

    lax.fori_loop(0, sends, take_u, 0)

    def back_copy(i, of_u):
        block = rows_of(i, ROWS)
        if of_u:
            return remote(normed_u.at[block], back_fast.at[block], send_back_sem.at[0, i], recv_back_fast_sem.at[i], fast_id)
        return remote(normed_w.at[block], back_slow.at[block], send_back_sem.at[1, i], recv_back_slow_sem.at[i], slow_id)

    def branch_w(i, carry):
        to_slow(i).wait_recv()
        block = rows_of(i, ROWS)
        x = jnp.where(has_slow, from_slow[block, :], own[block, :])
        put_query(block, x)
        put_key_value(block, x, k_w, v_even_w, v_odd_w)
        normed_w[block, :] = attend(block, x, k_u, v_even_u, v_odd_u)
        back_copy(i, False).start()
        return carry

    lax.fori_loop(0, steps, branch_w, 0)

    def branch_u(i, carry):
        block = rows_of(i, ROWS)
        x = x_u[block, :]
        put_query(block, x)
        normed_u[block, :] = attend(block, x, k_w, v_even_w, v_odd_w)
        back_copy(i, True).start()
        return carry

    lax.fori_loop(0, steps, branch_u, 0)

    for copy in conf_copies():
        copy.wait()
    parts = jnp.concatenate(
        [conf_fast[0:1, :], conf_slow[1:2, :], conf_out[2:4, :], jnp.zeros((4, tok), F32)], axis=0
    )
    weight = jnp.sum(parts, axis=0, keepdims=True)
    shares = jnp.transpose(parts / jnp.maximum(weight, 1.0))

    for i in range(steps):
        block = rows_of(i, ROWS)
        back_copy(i, True).wait_recv()
        back_copy(i, False).wait_recv()
        s = shares[i * ROWS : (i + 1) * ROWS, :]
        merged = s[:, 0:1] * back_fast[block, :].astype(F32)
        merged += s[:, 1:2] * back_slow[block, :].astype(F32)
        merged += s[:, 2:3] * normed_u[block, :].astype(F32)
        merged += s[:, 3:4] * normed_w[block, :].astype(F32)
        merged_ref[block, :] = merged.astype(BF16)

    for i in range(sends):
        to_fast(i).wait_send()
        to_slow(i).wait_send()
    for i in range(steps):
        back_copy(i, True).wait_send()
        back_copy(i, False).wait_send()


def merged_normed(mesh_shape, pair_list, confidence, tokens, w_embed, w_query, w_key, w_value, w_out, norm_gain):
    tok = tokens.shape[1]
    width = w_embed.shape[1]
    any_space = pl.BlockSpec(memory_space=pl.ANY)
    vmem = pl.BlockSpec(memory_space=pltpu.VMEM)
    rows = pltpu.VMEM((tok, width), BF16)
    return pl.pallas_call(
        functools.partial(kernel, mesh_shape),
        out_shape=jax.ShapeDtypeStruct((tok, width), BF16),
        in_specs=[pl.BlockSpec(memory_space=pltpu.SMEM), vmem, vmem] + [any_space] * 6,
        out_specs=vmem,
        scratch_shapes=[
            pltpu.VMEM(tokens.shape, BF16),
            pltpu.VMEM(w_embed.shape, BF16),
            pltpu.VMEM(w_query.shape, BF16),
            pltpu.VMEM(w_key.shape, BF16),
            pltpu.VMEM(w_value.shape, BF16),
            pltpu.VMEM(w_out.shape, BF16),
        ]
        + [rows] * 17
        + [pltpu.VMEM((8, tok), F32)] * 3
        + [
            pltpu.SemaphoreType.DMA((6,)),
            pltpu.SemaphoreType.DMA((2, tok // SEND_ROWS)),
            pltpu.SemaphoreType.DMA((tok // SEND_ROWS,)),
            pltpu.SemaphoreType.DMA((tok // SEND_ROWS,)),
            pltpu.SemaphoreType.DMA((2, tok // ROWS)),
            pltpu.SemaphoreType.DMA((tok // ROWS,)),
            pltpu.SemaphoreType.DMA((tok // ROWS,)),
            pltpu.SemaphoreType.DMA((4,)),
        ],
        compiler_params=pltpu.CompilerParams(
            collective_id=0, has_side_effects=True, vmem_limit_bytes=44 * 2**20
        ),
        name="pair_attention",
    )(pair_list, confidence, norm_gain[None], tokens, w_embed, w_query, w_key, w_value, w_out)


def solution(mesh):
    mesh_shape = (mesh.shape["group"], mesh.shape["dev"])

    def on_device(
        tokens, pair_list, confidence, w_embed, w_query, w_key, w_value, w_out, norm_gain, w_head
    ):
        merged = merged_normed(
            mesh_shape, pair_list, confidence, tokens, w_embed, w_query, w_key, w_value, w_out, norm_gain
        )
        return dot(merged, w_head).astype(BF16)[None]

    along = ("group", "dev")
    in_specs = (P(along, None, None), P(along, None), P(along, None, None)) + (P(),) * 7
    return jax.shard_map(
        on_device, mesh=mesh, in_specs=in_specs, out_specs=P(along, None, None), check_vma=False
    )
```

```python
import functools

import jax
import jax.numpy as jnp
from jax import lax
from jax.experimental import pallas as pl
from jax.experimental.pallas import tpu as pltpu
from jax.sharding import PartitionSpec as P

HEADS = 12
HEAD_DIM = 64
PAIRED = 2 * HEAD_DIM
LOG2E = 1.4426950408889634
MESH = pl.DeviceIdType.MESH
BF16 = jnp.bfloat16
F32 = jnp.float32
SEND_ROWS = 128
ROWS = 256
AHEAD = 2


def dot(a, b):
    return jnp.dot(a, b, preferred_element_type=F32)


def kernel(
    mesh_shape,
    pair_hbm,
    conf_hbm,
    gain_hbm,
    tokens_hbm,
    w_embed_hbm,
    w_query_hbm,
    w_key_hbm,
    w_value_hbm,
    w_out_hbm,
    merged_ref,
    pair_ref,
    conf_ref,
    gain_ref,
    tokens,
    w_embed,
    w_query,
    w_key,
    w_value,
    w_out,
    own,
    from_fast,
    from_slow,
    x_u,
    q_even_u,
    q_odd_u,
    q_even_w,
    q_odd_w,
    k_u,
    k_w,
    v_even_u,
    v_odd_u,
    v_even_w,
    v_odd_w,
    context,
    normed_u,
    normed_w,
    back_fast,
    back_slow,
    conf_out,
    conf_fast,
    conf_slow,
    load_sem,
    send_sem,
    recv_fast_sem,
    recv_slow_sem,
    send_back_sem,
    recv_back_fast_sem,
    recv_back_slow_sem,
    conf_sem,
):
    n_group, n_dev = mesh_shape
    n = n_group * n_dev
    me = lax.axis_index("group") * n_dev + lax.axis_index("dev")
    odd = lax.rem(me, 2)
    fast = me + 1 - 2 * odd
    slow = lax.rem(me + 2 * odd - 1 + n, n)
    fast_id = (lax.div(fast, n_dev), lax.rem(fast, n_dev))
    slow_id = (lax.div(slow, n_dev), lax.rem(slow, n_dev))
    tok = own.shape[0]
    sends = tok // SEND_ROWS
    steps = tok // ROWS

    def rows_of(step, size):
        return pl.ds(step * size, size)

    loads = [
        pltpu.make_async_copy(src, dst, load_sem.at[i])
        for i, (src, dst) in enumerate(
            (
                (w_embed_hbm, w_embed),
                (tokens_hbm.at[0], tokens),
                (pair_hbm, pair_ref),
                (conf_hbm, conf_ref),
                (gain_hbm, gain_ref),
                (w_key_hbm, w_key),
                (w_value_hbm, w_value),
                (w_query_hbm, w_query),
                (w_out_hbm, w_out),
            )
        )
    ]
    for load in loads[:5]:
        load.start()

    barrier = pltpu.get_barrier_semaphore()
    pl.semaphore_signal(barrier, inc=1, device_id=fast_id, device_id_type=MESH)
    pl.semaphore_signal(barrier, inc=1, device_id=slow_id, device_id_type=MESH)

    def remote(src, dst, send, recv, target):
        return pltpu.make_async_remote_copy(
            src_ref=src,
            dst_ref=dst,
            send_sem=send,
            recv_sem=recv,
            device_id=target,
            device_id_type=MESH,
        )

    def to_fast(i):
        block = rows_of(i, SEND_ROWS)
        return remote(own.at[block], from_fast.at[block], send_sem.at[0, i], recv_fast_sem.at[i], fast_id)

    def to_slow(i):
        block = rows_of(i, SEND_ROWS)
        return remote(own.at[block], from_slow.at[block], send_sem.at[1, i], recv_slow_sem.at[i], slow_id)

    def conf_copies():
        return (
            remote(conf_out, conf_fast, conf_sem.at[0], conf_sem.at[1], fast_id),
            remote(conf_out, conf_slow, conf_sem.at[2], conf_sem.at[3], slow_id),
        )

    for load in loads[:2]:
        load.wait()
    for load in loads[5:]:
        load.start()
    for begin, end in ((0, SEND_ROWS), (SEND_ROWS, tok)):
        own[begin:end, :] = dot(tokens[begin:end, :], w_embed[...]).astype(BF16)
        if begin == 0:
            pl.semaphore_wait(barrier, 2)
        for i in range(begin // SEND_ROWS, end // SEND_ROWS):
            to_slow(i).start()
        for i in range(begin // SEND_ROWS, end // SEND_ROWS):
            to_fast(i).start()

    for load in loads[2:5]:
        load.wait()
    first, second = pair_ref[0, 0], pair_ref[0, 1]
    has_fast = jnp.logical_or(first == fast, second == fast)
    has_slow = jnp.logical_or(first == slow, second == slow)
    u_image = jnp.where(has_fast, fast, me)
    u_first = (first == u_image).astype(F32)
    f_fast, f_slow = has_fast.astype(F32), has_slow.astype(F32)
    conf_first = conf_ref[0, 0:1, :].astype(F32)
    conf_second = conf_ref[0, 1:2, :].astype(F32)
    conf_u = conf_first * u_first + conf_second * (1.0 - u_first)
    conf_w = conf_second * u_first + conf_first * (1.0 - u_first)
    conf_out[...] = jnp.concatenate(
        [
            conf_u * f_fast,
            conf_w * f_slow,
            conf_u * (1.0 - f_fast),
            conf_w * (1.0 - f_slow),
            jnp.zeros((4, tok), F32),
        ],
        axis=0,
    )
    for copy in conf_copies():
        copy.start()

    lower_half = lax.broadcasted_iota(jnp.int32, (1, HEADS * HEAD_DIM), 1) % PAIRED < HEAD_DIM
    half = lax.broadcasted_iota(jnp.int32, (1, PAIRED), 1) < HEAD_DIM

    def put_query(block, x, even_ref, odd_ref):
        q = dot(x, w_query[...]) * (LOG2E / HEAD_DIM**0.5)
        even_ref[block, :] = jnp.where(lower_half, q, 0.0).astype(BF16)
        odd_ref[block, :] = jnp.where(lower_half, 0.0, q).astype(BF16)

    def put_key(block, x, k_ref):
        k_ref[block, :] = dot(x, w_key[...]).astype(BF16)

    def put_value(block, x, even_ref, odd_ref):
        v = dot(x, w_value[...])
        even_ref[block, :] = jnp.where(lower_half, v, 1.0).astype(BF16)
        odd_ref[block, :] = jnp.where(lower_half, 1.0, v).astype(BF16)

    def attend(block, x, q_refs, k_ref, v_refs):
        def lanes(h):
            return slice(h // 2 * PAIRED, (h // 2 + 1) * PAIRED)

        def scores_of(h):
            return lax.dot_general(
                q_refs[h % 2][block, lanes(h)],
                k_ref[:, lanes(h)],
                (((1,), (1,)), ((), ())),
                preferred_element_type=F32,
            )

        scores = {h: scores_of(h) for h in range(AHEAD)}
        for h in range(HEADS):
            if h + AHEAD < HEADS:
                scores[h + AHEAD] = scores_of(h + AHEAD)
            s = scores.pop(h)
            expo = jnp.exp2(s - jnp.max(s, axis=1, keepdims=True)).astype(BF16)
            result = dot(expo, v_refs[h % 2][:, lanes(h)])
            if h % 2 == 0:
                even = result
            else:
                total = jnp.where(half, even, result)
                weight = pltpu.roll(jnp.where(half, result, even), HEAD_DIM, 1)
                context[block, lanes(h)] = (total / weight).astype(BF16)
        mixed = x.astype(F32) + dot(context[block, :], w_out[...])
        center = mixed - jnp.mean(mixed, axis=-1, keepdims=True)
        spread = jnp.mean(center * center, axis=-1, keepdims=True)
        return (center * lax.rsqrt(spread + 1e-06) * gain_ref[...][None]).astype(BF16)

    for load in loads[5:]:
        load.wait()
    for i in range(sends):
        to_fast(i).wait_recv()
    every = slice(0, tok)
    x = jnp.where(has_fast, from_fast[...], own[...])
    x_u[...] = x
    put_key(every, x, k_u)
    put_value(every, x, v_even_u, v_odd_u)
    put_query(every, x, q_even_u, q_odd_u)

    def back_to_fast(i):
        block = rows_of(i, ROWS)
        return remote(normed_u.at[block], back_fast.at[block], send_back_sem.at[0, i], recv_back_fast_sem.at[i], fast_id)

    def back_to_slow(i):
        block = rows_of(i, ROWS)
        return remote(normed_w.at[block], back_slow.at[block], send_back_sem.at[1, i], recv_back_slow_sem.at[i], slow_id)

    for i in range(steps):
        for part in range(i * ROWS // SEND_ROWS, (i + 1) * ROWS // SEND_ROWS):
            to_slow(part).wait_recv()
        block = slice(i * ROWS, (i + 1) * ROWS)
        x = jnp.where(has_slow, from_slow[block, :], own[block, :])
        put_query(block, x, q_even_w, q_odd_w)
        put_key(block, x, k_w)
        put_value(block, x, v_even_w, v_odd_w)
        normed_w[block, :] = attend(block, x, (q_even_w, q_odd_w), k_u, (v_even_u, v_odd_u))
        back_to_slow(i).start()

    for i in range(steps):
        block = slice(i * ROWS, (i + 1) * ROWS)
        normed_u[block, :] = attend(block, x_u[block, :], (q_even_u, q_odd_u), k_w, (v_even_w, v_odd_w))
        back_to_fast(i).start()

    for copy in conf_copies():
        copy.wait()
    parts = jnp.concatenate(
        [conf_fast[0:1, :], conf_slow[1:2, :], conf_out[2:4, :], jnp.zeros((4, tok), F32)], axis=0
    )
    weight = jnp.sum(parts, axis=0, keepdims=True)
    shares = jnp.transpose(parts / jnp.maximum(weight, 1.0))

    for i in range(steps):
        block = slice(i * ROWS, (i + 1) * ROWS)
        back_to_fast(i).wait_recv()
        back_to_slow(i).wait_recv()
        s = shares[block, :]
        merged = s[:, 0:1] * back_fast[block, :].astype(F32)
        merged += s[:, 1:2] * back_slow[block, :].astype(F32)
        merged += s[:, 2:3] * normed_u[block, :].astype(F32)
        merged += s[:, 3:4] * normed_w[block, :].astype(F32)
        merged_ref[block, :] = merged.astype(BF16)

    for i in range(sends):
        to_fast(i).wait_send()
        to_slow(i).wait_send()
    for i in range(steps):
        back_to_fast(i).wait_send()
        back_to_slow(i).wait_send()


def merged_normed(mesh_shape, pair_list, confidence, tokens, w_embed, w_query, w_key, w_value, w_out, norm_gain):
    tok = tokens.shape[1]
    width = w_embed.shape[1]
    in_hbm = pl.BlockSpec(memory_space=pl.ANY)
    operands = (pair_list, confidence, norm_gain, tokens, w_embed, w_query, w_key, w_value, w_out)
    return pl.pallas_call(
        functools.partial(kernel, mesh_shape),
        out_shape=jax.ShapeDtypeStruct((tok, width), BF16),
        in_specs=[in_hbm] * len(operands),
        out_specs=pl.BlockSpec(memory_space=pltpu.VMEM),
        scratch_shapes=[
            pltpu.SMEM(pair_list.shape, jnp.int32),
            pltpu.VMEM(confidence.shape, jnp.int32),
            pltpu.VMEM(norm_gain.shape, F32),
            pltpu.VMEM(tokens.shape[1:], BF16),
            pltpu.VMEM(w_embed.shape, BF16),
            pltpu.VMEM(w_query.shape, BF16),
            pltpu.VMEM(w_key.shape, BF16),
            pltpu.VMEM(w_value.shape, BF16),
            pltpu.VMEM(w_out.shape, BF16),
        ]
        + [pltpu.VMEM((tok, width), BF16)] * 19
        + [pltpu.VMEM((8, tok), F32)] * 3
        + [
            pltpu.SemaphoreType.DMA((len(operands),)),
            pltpu.SemaphoreType.DMA((2, tok // SEND_ROWS)),
            pltpu.SemaphoreType.DMA((tok // SEND_ROWS,)),
            pltpu.SemaphoreType.DMA((tok // SEND_ROWS,)),
            pltpu.SemaphoreType.DMA((2, tok // ROWS)),
            pltpu.SemaphoreType.DMA((tok // ROWS,)),
            pltpu.SemaphoreType.DMA((tok // ROWS,)),
            pltpu.SemaphoreType.DMA((4,)),
        ],
        compiler_params=pltpu.CompilerParams(
            collective_id=0, has_side_effects=True, vmem_limit_bytes=48 * 2**20
        ),
        name="pair_attention",
    )(*(pltpu.with_memory_space_constraint(a, pltpu.HBM) for a in operands))


def solution(mesh):
    mesh_shape = (mesh.shape["group"], mesh.shape["dev"])

    def on_device(
        tokens, pair_list, confidence, w_embed, w_query, w_key, w_value, w_out, norm_gain, w_head
    ):
        merged = merged_normed(
            mesh_shape, pair_list, confidence, tokens, w_embed, w_query, w_key, w_value, w_out, norm_gain
        )
        return dot(merged, w_head).astype(BF16)[None]

    along = ("group", "dev")
    in_specs = (P(along, None, None), P(along, None), P(along, None, None)) + (P(),) * 7
    return jax.shard_map(
        on_device, mesh=mesh, in_specs=in_specs, out_specs=P(along, None, None), check_vma=False
    )
```

```python
import functools

import jax
import jax.numpy as jnp
from jax import lax
from jax.experimental import pallas as pl
from jax.experimental.pallas import tpu as pltpu
from jax.sharding import PartitionSpec as P

HEADS = 12
HEAD_DIM = 64
PAIRED = 2 * HEAD_DIM
LOG2E = 1.4426950408889634
MESH = pl.DeviceIdType.MESH
BF16 = jnp.bfloat16
F32 = jnp.float32
SEND_ROWS = 128
W_BLOCKS = ((0, 128), (128, 256), (256, 384), (384, 512))
U_BLOCKS = ((0, 256), (256, 512))
HEAD_BLOCKS = ((0, 256), (256, 384))
HEAD_ROWS = 384
HEAD_TILE = 512
FINISH_TILE = 1152


def dot(a, b):
    return jnp.dot(a, b, preferred_element_type=F32)


def kernel(
    mesh_shape,
    pair_hbm,
    conf_hbm,
    gain_hbm,
    tokens_hbm,
    w_embed_hbm,
    w_query_hbm,
    w_key_hbm,
    w_value_hbm,
    w_out_hbm,
    w_head_hbm,
    merged_ref,
    head_ref,
    w_head,
    pair_ref,
    conf_ref,
    gain_ref,
    tokens,
    w_embed,
    w_query,
    w_key,
    w_value,
    w_out,
    own,
    from_fast,
    from_slow,
    x_u,
    q_even_u,
    q_odd_u,
    q_even_w,
    q_odd_w,
    k_u,
    k_w,
    v_even_u,
    v_odd_u,
    v_even_w,
    v_odd_w,
    context,
    normed_u,
    normed_w,
    back_fast,
    back_slow,
    conf_out,
    conf_fast,
    conf_slow,
    load_sem,
    send_sem,
    recv_fast_sem,
    recv_slow_sem,
    send_back_sem,
    recv_back_fast_sem,
    recv_back_slow_sem,
    conf_sem,
):
    n_group, n_dev = mesh_shape
    n = n_group * n_dev
    me = lax.axis_index("group") * n_dev + lax.axis_index("dev")
    odd = lax.rem(me, 2)
    fast = me + 1 - 2 * odd
    slow = lax.rem(me + 2 * odd - 1 + n, n)
    fast_id = (lax.div(fast, n_dev), lax.rem(fast, n_dev))
    slow_id = (lax.div(slow, n_dev), lax.rem(slow, n_dev))
    tok = own.shape[0]
    sends = tok // SEND_ROWS
    chained = jnp.logical_and(slow != 0, me != 0)

    def rows_of(step, size):
        return pl.ds(step * size, size)

    loads = [
        pltpu.make_async_copy(src, dst, load_sem.at[i])
        for i, (src, dst) in enumerate(
            (
                (tokens_hbm.at[0, 0:SEND_ROWS], tokens.at[0:SEND_ROWS]),
                (w_embed_hbm, w_embed),
                (tokens_hbm.at[0, SEND_ROWS:tok], tokens.at[SEND_ROWS:tok]),
                (pair_hbm, pair_ref),
                (conf_hbm, conf_ref),
                (gain_hbm, gain_ref),
                (w_key_hbm, w_key),
                (w_value_hbm, w_value),
                (w_query_hbm, w_query),
                (w_out_hbm, w_out),
                (w_head_hbm, w_head),
            )
        )
    ]
    for load in loads[:6]:
        load.start()

    barrier = pltpu.get_barrier_semaphore()
    pl.semaphore_signal(barrier, inc=1, device_id=fast_id, device_id_type=MESH)

    @pl.when(chained)
    def _():
        pl.semaphore_signal(barrier, inc=1, device_id=slow_id, device_id_type=MESH)


    def remote(src, dst, send, recv, target):
        return pltpu.make_async_remote_copy(
            src_ref=src,
            dst_ref=dst,
            send_sem=send,
            recv_sem=recv,
            device_id=target,
            device_id_type=MESH,
        )

    def to_fast(i):
        block = rows_of(i, SEND_ROWS)
        return remote(own.at[block], from_fast.at[block], send_sem.at[0, i], recv_fast_sem.at[i], fast_id)

    def to_slow(i):
        block = rows_of(i, SEND_ROWS)
        return remote(own.at[block], from_slow.at[block], send_sem.at[1, i], recv_slow_sem.at[i], slow_id)

    def conf_to_fast():
        return remote(conf_out, conf_fast, conf_sem.at[0], conf_sem.at[1], fast_id)

    def conf_to_slow():
        return remote(conf_out, conf_slow, conf_sem.at[2], conf_sem.at[3], slow_id)

    for load in loads[:2]:
        load.wait()
    for load in loads[6:]:
        load.start()
    for begin, end in ((0, SEND_ROWS), (SEND_ROWS, tok)):
        if begin > 0:
            loads[2].wait()
        own[begin:end, :] = dot(tokens[begin:end, :], w_embed[...]).astype(BF16)
        if begin == 0:

            @pl.when(chained)
            def _():
                pl.semaphore_wait(barrier, 2)

            @pl.when(jnp.logical_not(chained))
            def _():
                pl.semaphore_wait(barrier, 1)
                from_slow[...] = jnp.zeros_like(from_slow)
                back_slow[...] = jnp.zeros_like(back_slow)
                conf_slow[...] = jnp.zeros_like(conf_slow)

        @pl.when(chained)
        def _(begin=begin, end=end):
            for i in range(begin // SEND_ROWS, end // SEND_ROWS):
                to_slow(i).start()

        for i in range(begin // SEND_ROWS, end // SEND_ROWS):
            to_fast(i).start()

    for load in loads[3:6]:
        load.wait()
    first, second = pair_ref[0, 0], pair_ref[0, 1]
    has_fast = jnp.logical_or(first == fast, second == fast)
    has_slow = jnp.logical_or(first == slow, second == slow)
    u_image = jnp.where(has_fast, fast, me)
    u_first = (first == u_image).astype(F32)
    f_fast, f_slow = has_fast.astype(F32), has_slow.astype(F32)
    conf_first = conf_ref[0, 0:1, :].astype(F32)
    conf_second = conf_ref[0, 1:2, :].astype(F32)
    conf_u = conf_first * u_first + conf_second * (1.0 - u_first)
    conf_w = conf_second * u_first + conf_first * (1.0 - u_first)
    conf_out[...] = jnp.concatenate(
        [
            conf_u * f_fast,
            conf_w * f_slow,
            conf_u * (1.0 - f_fast),
            conf_w * (1.0 - f_slow),
            jnp.zeros((4, tok), F32),
        ],
        axis=0,
    )
    conf_to_fast().start()

    @pl.when(chained)
    def _():
        conf_to_slow().start()


    lower_half = lax.broadcasted_iota(jnp.int32, (1, HEADS * HEAD_DIM), 1) % PAIRED < HEAD_DIM
    half = lax.broadcasted_iota(jnp.int32, (1, PAIRED), 1) < HEAD_DIM

    def put_query(block, x, even_ref, odd_ref):
        q = dot(x, w_query[...]) * (LOG2E / HEAD_DIM**0.5)
        even_ref[block, :] = jnp.where(lower_half, q, 0.0).astype(BF16)
        odd_ref[block, :] = jnp.where(lower_half, 0.0, q).astype(BF16)

    def put_key(block, x, k_ref):
        k_ref[block, :] = dot(x, w_key[...]).astype(BF16)

    def put_value(block, x, even_ref, odd_ref):
        v = dot(x, w_value[...])
        even_ref[block, :] = jnp.where(lower_half, v, 1.0).astype(BF16)
        odd_ref[block, :] = jnp.where(lower_half, 1.0, v).astype(BF16)

    def attend(block, x, q_refs, k_ref, v_refs, ahead):
        def lanes(h):
            return slice(h // 2 * PAIRED, (h // 2 + 1) * PAIRED)

        def scores_of(h):
            return lax.dot_general(
                q_refs[h % 2][block, lanes(h)],
                k_ref[:, lanes(h)],
                (((1,), (1,)), ((), ())),
                preferred_element_type=F32,
            )

        scores = {h: scores_of(h) for h in range(ahead)}
        for h in range(HEADS):
            if h + ahead < HEADS:
                scores[h + ahead] = scores_of(h + ahead)
            s = scores.pop(h)
            expo = jnp.exp2(s - jnp.max(s, axis=1, keepdims=True)).astype(BF16)
            result = dot(expo, v_refs[h % 2][:, lanes(h)])
            if h % 2 == 0:
                even = result
            else:
                total = jnp.where(half, even, result)
                weight = pltpu.roll(jnp.where(half, result, even), HEAD_DIM, 1)
                context[block, lanes(h)] = (total / weight).astype(BF16)
        mixed = x.astype(F32) + dot(context[block, :], w_out[...])
        center = mixed - jnp.mean(mixed, axis=-1, keepdims=True)
        spread = jnp.mean(center * center, axis=-1, keepdims=True)
        return (center * lax.rsqrt(spread + 1e-06) * gain_ref[...][None]).astype(BF16)

    for load in loads[6:10]:
        load.wait()
    for i in range(sends):
        to_fast(i).wait_recv()
    every = slice(0, tok)
    x = jnp.where(has_fast, from_fast[...], own[...])
    x_u[...] = x
    put_key(every, x, k_u)
    put_value(every, x, v_even_u, v_odd_u)
    put_query(every, x, q_even_u, q_odd_u)

    def back_to_fast(i):
        block = pl.ds(U_BLOCKS[i][0], U_BLOCKS[i][1] - U_BLOCKS[i][0])
        return remote(normed_u.at[block], back_fast.at[block], send_back_sem.at[0, i], recv_back_fast_sem.at[i], fast_id)

    def back_to_slow(i):
        block = pl.ds(W_BLOCKS[i][0], W_BLOCKS[i][1] - W_BLOCKS[i][0])
        return remote(normed_w.at[block], back_slow.at[block], send_back_sem.at[1, i], recv_back_slow_sem.at[i], slow_id)

    for i, (begin, end) in enumerate(W_BLOCKS):

        @pl.when(chained)
        def _(begin=begin, end=end):
            for part in range(begin // SEND_ROWS, end // SEND_ROWS):
                to_slow(part).wait_recv()

        block = slice(begin, end)
        x = jnp.where(has_slow, from_slow[block, :], own[block, :])
        put_query(block, x, q_even_w, q_odd_w)
        put_key(block, x, k_w)
        put_value(block, x, v_even_w, v_odd_w)
        normed_w[block, :] = attend(block, x, (q_even_w, q_odd_w), k_u, (v_even_u, v_odd_u), 512 // (end - begin))

        @pl.when(chained)
        def _(i=i):
            back_to_slow(i).start()

    for i, (begin, end) in enumerate(U_BLOCKS):
        block = slice(begin, end)
        normed_u[block, :] = attend(
            block, x_u[block, :], (q_even_u, q_odd_u), k_w, (v_even_w, v_odd_w), 512 // (end - begin)
        )
        back_to_fast(i).start()

    loads[10].wait()
    conf_to_fast().wait()

    @pl.when(chained)
    def _():
        conf_to_slow().wait()

    parts = jnp.concatenate(
        [conf_fast[0:1, :], conf_slow[1:2, :], conf_out[2:4, :], jnp.zeros((4, tok), F32)], axis=0
    )
    weight = jnp.sum(parts, axis=0, keepdims=True)
    shares = jnp.transpose(parts / jnp.maximum(weight, 1.0))

    fast_here, slow_here = 0, 0
    for begin, end in HEAD_BLOCKS + ((HEAD_ROWS, tok),):
        block = slice(begin, end)
        while fast_here < len(U_BLOCKS) and U_BLOCKS[fast_here][0] < end:
            back_to_fast(fast_here).wait_recv()
            fast_here += 1
        behind = slow_here
        while slow_here < len(W_BLOCKS) and W_BLOCKS[slow_here][0] < end:
            slow_here += 1

        @pl.when(chained)
        def _(behind=behind, slow_here=slow_here):
            for i in range(behind, slow_here):
                back_to_slow(i).wait_recv()

        s = shares[block, :]
        merged = s[:, 0:1] * back_fast[block, :].astype(F32)
        merged += s[:, 1:2] * back_slow[block, :].astype(F32)
        merged += s[:, 2:3] * normed_u[block, :].astype(F32)
        merged += s[:, 3:4] * normed_w[block, :].astype(F32)
        merged = merged.astype(BF16)
        if begin < HEAD_ROWS:
            for left in range(0, w_head.shape[1], HEAD_TILE):
                tile = slice(left, min(left + HEAD_TILE, w_head.shape[1]))
                head_ref[block, tile] = dot(merged, w_head[:, tile]).astype(BF16)
        else:
            merged_ref[...] = merged

    for i in range(sends):
        to_fast(i).wait_send()
    for i in range(len(U_BLOCKS)):
        back_to_fast(i).wait_send()

    @pl.when(chained)
    def _():
        for i in range(sends):
            to_slow(i).wait_send()
        for i in range(len(W_BLOCKS)):
            back_to_slow(i).wait_send()


def merged_normed(mesh_shape, pair_list, confidence, tokens, w_embed, w_query, w_key, w_value, w_out, norm_gain, w_head):
    tok = tokens.shape[1]
    width = w_embed.shape[1]
    in_hbm = pl.BlockSpec(memory_space=pl.ANY)
    operands = (pair_list, confidence, norm_gain, tokens, w_embed, w_query, w_key, w_value, w_out, w_head)
    return pl.pallas_call(
        functools.partial(kernel, mesh_shape),
        out_shape=(
            jax.ShapeDtypeStruct((tok - HEAD_ROWS, width), BF16),
            jax.ShapeDtypeStruct((HEAD_ROWS, w_head.shape[1]), BF16),
            jax.ShapeDtypeStruct(w_head.shape, BF16),
        ),
        in_specs=[in_hbm] * len(operands),
        out_specs=[pl.BlockSpec(memory_space=pltpu.VMEM)] * 3,
        scratch_shapes=[
            pltpu.SMEM(pair_list.shape, jnp.int32),
            pltpu.VMEM(confidence.shape, jnp.int32),
            pltpu.VMEM(norm_gain.shape, F32),
            pltpu.VMEM(tokens.shape[1:], BF16),
            pltpu.VMEM(w_embed.shape, BF16),
            pltpu.VMEM(w_query.shape, BF16),
            pltpu.VMEM(w_key.shape, BF16),
            pltpu.VMEM(w_value.shape, BF16),
            pltpu.VMEM(w_out.shape, BF16),
        ]
        + [pltpu.VMEM((tok, width), BF16)] * 19
        + [pltpu.VMEM((8, tok), F32)] * 3
        + [
            pltpu.SemaphoreType.DMA((len(operands) + 1,)),
            pltpu.SemaphoreType.DMA((2, tok // SEND_ROWS)),
            pltpu.SemaphoreType.DMA((tok // SEND_ROWS,)),
            pltpu.SemaphoreType.DMA((tok // SEND_ROWS,)),
            pltpu.SemaphoreType.DMA((2, len(W_BLOCKS))),
            pltpu.SemaphoreType.DMA((len(U_BLOCKS),)),
            pltpu.SemaphoreType.DMA((len(W_BLOCKS),)),
            pltpu.SemaphoreType.DMA((4,)),
        ],
        compiler_params=pltpu.CompilerParams(
            collective_id=0, has_side_effects=True, vmem_limit_bytes=40 * 2**20
        ),
        name="pair_attention",
    )(*(pltpu.with_memory_space_constraint(a, pltpu.HBM) for a in operands))


def finish_kernel(merged_ref, head_ref, w_head, out_ref, last, copy_sem):
    copy = pltpu.make_async_copy(head_ref, out_ref.at[0, 0:HEAD_ROWS], copy_sem.at[0])
    copy.start()
    copies = [copy]
    width = w_head.shape[1]
    for i, left in enumerate(range(0, width, FINISH_TILE)):
        tile = slice(left, min(left + FINISH_TILE, width))
        last[:, tile] = dot(merged_ref[...], w_head[:, tile]).astype(BF16)
        copy = pltpu.make_async_copy(
            last.at[:, tile], out_ref.at[0, HEAD_ROWS : out_ref.shape[1], tile], copy_sem.at[1 + i]
        )
        copy.start()
        copies.append(copy)
    for copy in copies:
        copy.wait()


def finished(merged, head, w_head):
    tok, width = merged.shape[0] + head.shape[0], w_head.shape[1]
    return pl.pallas_call(
        finish_kernel,
        out_shape=jax.ShapeDtypeStruct((1, tok, width), BF16),
        in_specs=[pl.BlockSpec(memory_space=pltpu.VMEM)] * 3,
        out_specs=pl.BlockSpec(memory_space=pltpu.HBM),
        scratch_shapes=[
            pltpu.VMEM((merged.shape[0], width), BF16),
            pltpu.SemaphoreType.DMA((1 + -(-width // FINISH_TILE),)),
        ],
        compiler_params=pltpu.CompilerParams(vmem_limit_bytes=16 * 2**20),
        name="head_of_last_rows",
    )(merged, head, w_head)


def solution(mesh):
    mesh_shape = (mesh.shape["group"], mesh.shape["dev"])

    def on_device(
        tokens, pair_list, confidence, w_embed, w_query, w_key, w_value, w_out, norm_gain, w_head
    ):
        return finished(
            *merged_normed(
                mesh_shape, pair_list, confidence, tokens, w_embed, w_query, w_key, w_value, w_out, norm_gain, w_head
            )
        )

    along = ("group", "dev")
    in_specs = (P(along, None, None), P(along, None), P(along, None, None)) + (P(),) * 7
    return jax.shard_map(
        on_device, mesh=mesh, in_specs=in_specs, out_specs=P(along, None, None), check_vma=False
    )
```

```python
import functools

import jax
import jax.numpy as jnp
from jax import lax
from jax.experimental import pallas as pl
from jax.experimental.pallas import tpu as pltpu
from jax.sharding import PartitionSpec as P

HEADS = 12
HEAD_DIM = 64
PAIRED = 2 * HEAD_DIM
LOG2E = 1.4426950408889634
MESH = pl.DeviceIdType.MESH
BF16 = jnp.bfloat16
F32 = jnp.float32
SEND_ROWS = 128
EMBED_BLOCKS = ((0, 128), (128, 256), (256, 512))
TAKE_BLOCKS = ((0, 256), (256, 512))
W_BLOCKS = ((0, 128), (128, 256), (256, 384), (384, 512))
EARLY_KEYS = 256
U_BLOCKS = ((0, 256), (256, 512))
HEAD_BLOCKS = ((0, 256), (256, 384))
HEAD_ROWS = 384
HEAD_TILE = 512
FINISH_TILE = 1152


def dot(a, b):
    return jnp.dot(a, b, preferred_element_type=F32)


def kernel(
    mesh_shape,
    pair_hbm,
    conf_hbm,
    gain_hbm,
    tokens_hbm,
    w_embed_hbm,
    w_query_hbm,
    w_key_hbm,
    w_value_hbm,
    w_out_hbm,
    w_head_hbm,
    merged_ref,
    head_ref,
    w_head,
    pair_ref,
    conf_ref,
    gain_ref,
    tokens,
    w_embed,
    w_query,
    w_key,
    w_value,
    w_out,
    own,
    from_fast,
    from_slow,
    x_u,
    x_w,
    q_even_u,
    q_odd_u,
    q_even_w,
    q_odd_w,
    k_u,
    k_w,
    v_u,
    v_w,
    context,
    normed_u,
    normed_w,
    back_fast,
    back_slow,
    early_total,
    early_weight,
    early_top,
    conf_out,
    conf_fast,
    conf_slow,
    load_sem,
    send_sem,
    recv_fast_sem,
    recv_slow_sem,
    send_back_sem,
    recv_back_fast_sem,
    recv_back_slow_sem,
    conf_sem,
):
    n_group, n_dev = mesh_shape
    n = n_group * n_dev
    me = lax.axis_index("group") * n_dev + lax.axis_index("dev")
    odd = lax.rem(me, 2)
    fast = me + 1 - 2 * odd
    slow = lax.rem(me + 2 * odd - 1 + n, n)
    fast_id = (lax.div(fast, n_dev), lax.rem(fast, n_dev))
    slow_id = (lax.div(slow, n_dev), lax.rem(slow, n_dev))
    tok = own.shape[0]
    sends = tok // SEND_ROWS
    chained = jnp.logical_and(slow != 0, me != 0)

    def rows_of(step, size):
        return pl.ds(step * size, size)

    loads = [
        pltpu.make_async_copy(src, dst, load_sem.at[i])
        for i, (src, dst) in enumerate(
            (
                (tokens_hbm.at[0, 0:SEND_ROWS], tokens.at[0:SEND_ROWS]),
                (w_embed_hbm, w_embed),
                (tokens_hbm.at[0, SEND_ROWS:tok], tokens.at[SEND_ROWS:tok]),
                (pair_hbm, pair_ref),
                (conf_hbm, conf_ref),
                (gain_hbm, gain_ref),
                (w_key_hbm, w_key),
                (w_value_hbm, w_value),
                (w_query_hbm, w_query),
                (w_out_hbm, w_out),
                (w_head_hbm, w_head),
            )
        )
    ]
    for load in loads[:6]:
        load.start()

    barrier = pltpu.get_barrier_semaphore()
    pl.semaphore_signal(barrier, inc=1, device_id=fast_id, device_id_type=MESH)

    @pl.when(chained)
    def _():
        pl.semaphore_signal(barrier, inc=1, device_id=slow_id, device_id_type=MESH)


    def remote(src, dst, send, recv, target):
        return pltpu.make_async_remote_copy(
            src_ref=src,
            dst_ref=dst,
            send_sem=send,
            recv_sem=recv,
            device_id=target,
            device_id_type=MESH,
        )

    def to_fast(i):
        block = rows_of(i, SEND_ROWS)
        return remote(own.at[block], from_fast.at[block], send_sem.at[0, i], recv_fast_sem.at[i], fast_id)

    def to_slow(i):
        block = rows_of(i, SEND_ROWS)
        return remote(own.at[block], from_slow.at[block], send_sem.at[1, i], recv_slow_sem.at[i], slow_id)

    def conf_to_fast():
        return remote(conf_out, conf_fast, conf_sem.at[0], conf_sem.at[1], fast_id)

    def conf_to_slow():
        return remote(conf_out, conf_slow, conf_sem.at[2], conf_sem.at[3], slow_id)

    for load in loads[:2]:
        load.wait()
    for load in loads[6:]:
        load.start()
    for begin, end in EMBED_BLOCKS:
        if begin == SEND_ROWS:
            loads[2].wait()
        own[begin:end, :] = dot(tokens[begin:end, :], w_embed[...]).astype(BF16)
        if begin == 0:

            @pl.when(chained)
            def _():
                pl.semaphore_wait(barrier, 2)

            @pl.when(jnp.logical_not(chained))
            def _():
                pl.semaphore_wait(barrier, 1)
                from_slow[...] = jnp.zeros_like(from_slow)
                back_slow[...] = jnp.zeros_like(back_slow)
                conf_slow[...] = jnp.zeros_like(conf_slow)

        @pl.when(chained)
        def _(begin=begin, end=end):
            for i in range(begin // SEND_ROWS, end // SEND_ROWS):
                to_slow(i).start()

        for i in range(begin // SEND_ROWS, end // SEND_ROWS):
            to_fast(i).start()

    for load in loads[3:6]:
        load.wait()
    first, second = pair_ref[0, 0], pair_ref[0, 1]
    has_fast = jnp.logical_or(first == fast, second == fast)
    has_slow = jnp.logical_or(first == slow, second == slow)
    u_image = jnp.where(has_fast, fast, me)
    u_first = (first == u_image).astype(F32)
    f_fast, f_slow = has_fast.astype(F32), has_slow.astype(F32)
    conf_first = conf_ref[0, 0:1, :].astype(F32)
    conf_second = conf_ref[0, 1:2, :].astype(F32)
    conf_u = conf_first * u_first + conf_second * (1.0 - u_first)
    conf_w = conf_second * u_first + conf_first * (1.0 - u_first)
    conf_out[...] = jnp.concatenate(
        [
            conf_u * f_fast,
            conf_w * f_slow,
            conf_u * (1.0 - f_fast),
            conf_w * (1.0 - f_slow),
            jnp.zeros((4, tok), F32),
        ],
        axis=0,
    )
    conf_to_fast().start()

    @pl.when(chained)
    def _():
        conf_to_slow().start()


    lower_half = lax.broadcasted_iota(jnp.int32, (1, HEADS * HEAD_DIM), 1) % PAIRED < HEAD_DIM
    half = lax.broadcasted_iota(jnp.int32, (1, PAIRED), 1) < HEAD_DIM

    def put_query(block, x, even_ref, odd_ref):
        q = dot(x, w_query[...]) * (LOG2E / HEAD_DIM**0.5)
        even_ref[block, :] = jnp.where(lower_half, q, 0.0).astype(BF16)
        odd_ref[block, :] = jnp.where(lower_half, 0.0, q).astype(BF16)

    def put_key(block, x, k_ref):
        k_ref[block, :] = dot(x, w_key[...]).astype(BF16)

    def put_value(block, x, v_ref):
        v_ref[block, :] = dot(x, w_value[...]).astype(BF16)

    ones = jnp.ones((tok, PAIRED), BF16)

    def lanes(h):
        return slice(h // 2 * PAIRED, (h // 2 + 1) * PAIRED)

    class Attention:
        def __init__(self, block, x_ref, q_refs, k_ref, v_ref, keys):
            self.block, self.keys = slice(*block), slice(*keys)
            self.ahead = 512 * 512 // ((block[1] - block[0]) * (keys[1] - keys[0]))
            self.x_ref, self.q_refs, self.k_ref, self.v_ref = x_ref, q_refs, k_ref, v_ref
            self.scores = {h: self.scores_of(h) for h in range(self.ahead)}

        def scores_of(self, h):
            return lax.dot_general(
                self.q_refs[h % 2][self.block, lanes(h)],
                self.k_ref[self.keys, lanes(h)],
                (((1,), (1,)), ((), ())),
                preferred_element_type=F32,
            )

        def heads(self, early=False, late=False):
            for h in range(HEADS):
                if h + self.ahead < HEADS:
                    self.scores[h + self.ahead] = self.scores_of(h + self.ahead)
                s = self.scores.pop(h)
                top = jnp.max(s, axis=1, keepdims=True)
                if early or late:
                    top = jnp.broadcast_to(top, (s.shape[0], PAIRED))
                    if late:
                        before = early_top[h, self.block, :]
                        top = jnp.maximum(top, before)
                        scale = jnp.exp2(before - top)
                    else:
                        early_top[h, self.block, :] = top
                    top = jnp.concatenate([top] * (s.shape[1] // PAIRED), axis=1)
                expo = jnp.exp2(s - top).astype(BF16)
                values = jnp.concatenate([self.v_ref[self.keys, lanes(h)], ones[: s.shape[1]]], axis=1)
                result = dot(expo, values)
                if h % 2 == 0:
                    even, even_scale = result, scale if late else None
                    continue
                total = jnp.where(half, even[:, :PAIRED], result[:, :PAIRED])
                weight = jnp.where(half, even[:, PAIRED:], result[:, PAIRED:])
                if early:
                    early_total[h // 2, self.block, :] = total
                    early_weight[h // 2, self.block, :] = weight
                    continue
                if late:
                    scale = jnp.where(half, even_scale, scale)
                    total += early_total[h // 2, self.block, :] * scale
                    weight += early_weight[h // 2, self.block, :] * scale
                context[self.block, lanes(h)] = (total / weight).astype(BF16)

        def normed(self):
            mixed = self.x_ref[self.block, :].astype(F32) + dot(context[self.block, :], w_out[...])
            center = mixed - jnp.mean(mixed, axis=-1, keepdims=True)
            spread = jnp.mean(center * center, axis=-1, keepdims=True)
            return (center * lax.rsqrt(spread + 1e-06) * gain_ref[...][None]).astype(BF16)

    for load in loads[6:10]:
        load.wait()
    for begin, end in TAKE_BLOCKS:
        for i in range(begin // SEND_ROWS, end // SEND_ROWS):
            to_fast(i).wait_recv()
        block = slice(begin, end)
        x = jnp.where(has_fast, from_fast[block, :], own[block, :])
        x_u[block, :] = x
        put_key(block, x, k_u)
        put_value(block, x, v_u)
        put_query(block, x, q_even_u, q_odd_u)

    def back_to_fast(i):
        block = pl.ds(U_BLOCKS[i][0], U_BLOCKS[i][1] - U_BLOCKS[i][0])
        return remote(normed_u.at[block], back_fast.at[block], send_back_sem.at[0, i], recv_back_fast_sem.at[i], fast_id)

    def back_to_slow(i):
        block = pl.ds(W_BLOCKS[i][0], W_BLOCKS[i][1] - W_BLOCKS[i][0])
        return remote(normed_w.at[block], back_slow.at[block], send_back_sem.at[1, i], recv_back_slow_sem.at[i], slow_id)

    def end_w(i, attention):
        normed_w[attention.block, :] = attention.normed()

        @pl.when(chained)
        def _():
            back_to_slow(i).start()

    pending = None
    for i, (begin, end) in enumerate(W_BLOCKS):

        @pl.when(chained)
        def _(begin=begin, end=end):
            for part in range(begin // SEND_ROWS, end // SEND_ROWS):
                to_slow(part).wait_recv()

        block = slice(begin, end)
        x = jnp.where(has_slow, from_slow[block, :], own[block, :])
        x_w[block, :] = x
        put_query(block, x, q_even_w, q_odd_w)
        put_key(block, x, k_w)
        put_value(block, x, v_w)
        if pending is not None:
            end_w(i - 1, pending)
        pending = Attention((begin, end), x_w, (q_even_w, q_odd_w), k_u, v_u, (0, tok))
        pending.heads()
        if end == EARLY_KEYS:
            early = Attention((0, tok), x_u, (q_even_u, q_odd_u), k_w, v_w, (0, EARLY_KEYS))
            end_w(i, pending)
            pending = None
            early.heads(early=True)

    attentions = []
    for i, block in enumerate(U_BLOCKS):
        attentions.append(
            Attention(block, x_u, (q_even_u, q_odd_u), k_w, v_w, (EARLY_KEYS, tok))
        )
        if i == 0:
            end_w(len(W_BLOCKS) - 1, pending)
        else:
            normed_u[attentions[i - 1].block, :] = attentions[i - 1].normed()
            back_to_fast(i - 1).start()
        attentions[i].heads(late=True)
    normed_u[attentions[-1].block, :] = attentions[-1].normed()
    back_to_fast(len(U_BLOCKS) - 1).start()

    loads[10].wait()
    conf_to_fast().wait()

    @pl.when(chained)
    def _():
        conf_to_slow().wait()

    parts = jnp.concatenate(
        [conf_fast[0:1, :], conf_slow[1:2, :], conf_out[2:4, :], jnp.zeros((4, tok), F32)], axis=0
    )
    weight = jnp.sum(parts, axis=0, keepdims=True)
    shares = jnp.transpose(parts / jnp.maximum(weight, 1.0))

    fast_here, slow_here = 0, 0
    for begin, end in HEAD_BLOCKS + ((HEAD_ROWS, tok),):
        block = slice(begin, end)
        while fast_here < len(U_BLOCKS) and U_BLOCKS[fast_here][0] < end:
            back_to_fast(fast_here).wait_recv()
            fast_here += 1
        behind = slow_here
        while slow_here < len(W_BLOCKS) and W_BLOCKS[slow_here][0] < end:
            slow_here += 1

        @pl.when(chained)
        def _(behind=behind, slow_here=slow_here):
            for i in range(behind, slow_here):
                back_to_slow(i).wait_recv()

        s = shares[block, :]
        merged = s[:, 0:1] * back_fast[block, :].astype(F32)
        merged += s[:, 1:2] * back_slow[block, :].astype(F32)
        merged += s[:, 2:3] * normed_u[block, :].astype(F32)
        merged += s[:, 3:4] * normed_w[block, :].astype(F32)
        merged = merged.astype(BF16)
        if begin < HEAD_ROWS:
            for left in range(0, w_head.shape[1], HEAD_TILE):
                tile = slice(left, min(left + HEAD_TILE, w_head.shape[1]))
                head_ref[block, tile] = dot(merged, w_head[:, tile]).astype(BF16)
        else:
            merged_ref[...] = merged

    for i in range(sends):
        to_fast(i).wait_send()
    for i in range(len(U_BLOCKS)):
        back_to_fast(i).wait_send()

    @pl.when(chained)
    def _():
        for i in range(sends):
            to_slow(i).wait_send()
        for i in range(len(W_BLOCKS)):
            back_to_slow(i).wait_send()


def merged_normed(mesh_shape, pair_list, confidence, tokens, w_embed, w_query, w_key, w_value, w_out, norm_gain, w_head):
    tok = tokens.shape[1]
    width = w_embed.shape[1]
    in_hbm = pl.BlockSpec(memory_space=pl.ANY)
    operands = (pair_list, confidence, norm_gain, tokens, w_embed, w_query, w_key, w_value, w_out, w_head)
    return pl.pallas_call(
        functools.partial(kernel, mesh_shape),
        out_shape=(
            jax.ShapeDtypeStruct((tok - HEAD_ROWS, width), BF16),
            jax.ShapeDtypeStruct((HEAD_ROWS, w_head.shape[1]), BF16),
            jax.ShapeDtypeStruct(w_head.shape, BF16),
        ),
        in_specs=[in_hbm] * len(operands),
        out_specs=[pl.BlockSpec(memory_space=pltpu.VMEM)] * 3,
        scratch_shapes=[
            pltpu.SMEM(pair_list.shape, jnp.int32),
            pltpu.VMEM(confidence.shape, jnp.int32),
            pltpu.VMEM(norm_gain.shape, F32),
            pltpu.VMEM(tokens.shape[1:], BF16),
            pltpu.VMEM(w_embed.shape, BF16),
            pltpu.VMEM(w_query.shape, BF16),
            pltpu.VMEM(w_key.shape, BF16),
            pltpu.VMEM(w_value.shape, BF16),
            pltpu.VMEM(w_out.shape, BF16),
        ]
        + [pltpu.VMEM((tok, width), BF16)] * 18
        + [pltpu.VMEM((HEADS // 2, tok, PAIRED), F32)] * 2
        + [pltpu.VMEM((HEADS, tok, PAIRED), F32)]
        + [pltpu.VMEM((8, tok), F32)] * 3
        + [
            pltpu.SemaphoreType.DMA((len(operands) + 1,)),
            pltpu.SemaphoreType.DMA((2, tok // SEND_ROWS)),
            pltpu.SemaphoreType.DMA((tok // SEND_ROWS,)),
            pltpu.SemaphoreType.DMA((tok // SEND_ROWS,)),
            pltpu.SemaphoreType.DMA((2, len(W_BLOCKS))),
            pltpu.SemaphoreType.DMA((len(U_BLOCKS),)),
            pltpu.SemaphoreType.DMA((len(W_BLOCKS),)),
            pltpu.SemaphoreType.DMA((4,)),
        ],
        compiler_params=pltpu.CompilerParams(
            collective_id=0, has_side_effects=True, vmem_limit_bytes=40 * 2**20
        ),
        name="pair_attention",
    )(*(pltpu.with_memory_space_constraint(a, pltpu.HBM) for a in operands))


def finish_kernel(merged_ref, head_ref, w_head, out_ref, last, copy_sem):
    copy = pltpu.make_async_copy(head_ref, out_ref.at[0, 0:HEAD_ROWS], copy_sem.at[0])
    copy.start()
    copies = [copy]
    width = w_head.shape[1]
    for i, left in enumerate(range(0, width, FINISH_TILE)):
        tile = slice(left, min(left + FINISH_TILE, width))
        last[:, tile] = dot(merged_ref[...], w_head[:, tile]).astype(BF16)
        copy = pltpu.make_async_copy(
            last.at[:, tile], out_ref.at[0, HEAD_ROWS : out_ref.shape[1], tile], copy_sem.at[1 + i]
        )
        copy.start()
        copies.append(copy)
    for copy in copies:
        copy.wait()


def finished(merged, head, w_head):
    tok, width = merged.shape[0] + head.shape[0], w_head.shape[1]
    return pl.pallas_call(
        finish_kernel,
        out_shape=jax.ShapeDtypeStruct((1, tok, width), BF16),
        in_specs=[pl.BlockSpec(memory_space=pltpu.VMEM)] * 3,
        out_specs=pl.BlockSpec(memory_space=pltpu.HBM),
        scratch_shapes=[
            pltpu.VMEM((merged.shape[0], width), BF16),
            pltpu.SemaphoreType.DMA((1 + -(-width // FINISH_TILE),)),
        ],
        compiler_params=pltpu.CompilerParams(vmem_limit_bytes=16 * 2**20),
        name="head_of_last_rows",
    )(merged, head, w_head)


def solution(mesh):
    mesh_shape = (mesh.shape["group"], mesh.shape["dev"])

    def on_device(
        tokens, pair_list, confidence, w_embed, w_query, w_key, w_value, w_out, norm_gain, w_head
    ):
        return finished(
            *merged_normed(
                mesh_shape, pair_list, confidence, tokens, w_embed, w_query, w_key, w_value, w_out, norm_gain, w_head
            )
        )

    along = ("group", "dev")
    in_specs = (P(along, None, None), P(along, None), P(along, None, None)) + (P(),) * 7
    return jax.shard_map(
        on_device, mesh=mesh, in_specs=in_specs, out_specs=P(along, None, None), check_vma=False
    )
```

```python
import functools

import jax
import jax.numpy as jnp
from jax import lax
from jax.experimental import pallas as pl
from jax.experimental.pallas import tpu as pltpu
from jax.sharding import PartitionSpec as P

HEADS = 12
HEAD_DIM = 64
PAIRED = 2 * HEAD_DIM
LOG2E = 1.4426950408889634
MESH = pl.DeviceIdType.MESH
BF16 = jnp.bfloat16
F32 = jnp.float32
SEND_ROWS = 128
EMBED_BLOCKS = ((0, 128), (128, 256), (256, 512))
TAKE_BLOCKS = ((0, 256), (256, 512))
W_BLOCKS = ((0, 128), (128, 256), (256, 384), (384, 512))
U_BLOCKS = ((0, 256), (256, 512))
HEAD_BLOCKS = ((0, 256), (256, 384))
HEAD_ROWS = 384
HEAD_TILE = 512
FINISH_TILE = 1152


def dot(a, b):
    return jnp.dot(a, b, preferred_element_type=F32)


def kernel(
    mesh_shape,
    pair_hbm,
    conf_hbm,
    gain_hbm,
    tokens_hbm,
    w_embed_hbm,
    w_query_hbm,
    w_key_hbm,
    w_value_hbm,
    w_out_hbm,
    w_head_hbm,
    merged_ref,
    head_ref,
    w_head,
    pair_ref,
    conf_ref,
    gain_ref,
    tokens,
    w_embed,
    w_query,
    w_key,
    w_value,
    w_out,
    own,
    from_fast,
    from_slow,
    x_u,
    x_w,
    q_even_u,
    q_odd_u,
    q_even_w,
    q_odd_w,
    k_u,
    k_w,
    v_u,
    v_w,
    context,
    normed_u,
    normed_w,
    back_fast,
    back_slow,
    conf_out,
    conf_fast,
    conf_slow,
    load_sem,
    send_sem,
    recv_fast_sem,
    recv_slow_sem,
    send_back_sem,
    recv_back_fast_sem,
    recv_back_slow_sem,
    conf_sem,
):
    n_group, n_dev = mesh_shape
    n = n_group * n_dev
    me = lax.axis_index("group") * n_dev + lax.axis_index("dev")
    odd = lax.rem(me, 2)
    fast = me + 1 - 2 * odd
    slow = lax.rem(me + 2 * odd - 1 + n, n)
    fast_id = (lax.div(fast, n_dev), lax.rem(fast, n_dev))
    slow_id = (lax.div(slow, n_dev), lax.rem(slow, n_dev))
    tok = own.shape[0]
    sends = tok // SEND_ROWS
    chained = jnp.logical_and(slow != 0, me != 0)

    def rows_of(step, size):
        return pl.ds(step * size, size)

    first_rows = EMBED_BLOCKS[0][1]
    loads = [
        pltpu.make_async_copy(src, dst, load_sem.at[i])
        for i, (src, dst) in enumerate(
            (
                (tokens_hbm.at[0, 0:first_rows], tokens.at[0:first_rows]),
                (w_embed_hbm, w_embed),
                (tokens_hbm.at[0, first_rows:tok], tokens.at[first_rows:tok]),
                (pair_hbm, pair_ref),
                (conf_hbm, conf_ref),
                (gain_hbm, gain_ref),
                (w_key_hbm, w_key),
                (w_value_hbm, w_value),
                (w_query_hbm, w_query),
                (w_out_hbm, w_out),
                (w_head_hbm, w_head),
            )
        )
    ]
    for load in loads[:6]:
        load.start()

    barrier = pltpu.get_barrier_semaphore()
    pl.semaphore_signal(barrier, inc=1, device_id=fast_id, device_id_type=MESH)

    @pl.when(chained)
    def _():
        pl.semaphore_signal(barrier, inc=1, device_id=slow_id, device_id_type=MESH)


    def remote(src, dst, send, recv, target):
        return pltpu.make_async_remote_copy(
            src_ref=src,
            dst_ref=dst,
            send_sem=send,
            recv_sem=recv,
            device_id=target,
            device_id_type=MESH,
        )

    def to_fast(i):
        block = rows_of(i, SEND_ROWS)
        return remote(own.at[block], from_fast.at[block], send_sem.at[0, i], recv_fast_sem.at[i], fast_id)

    def to_slow(i):
        block = rows_of(i, SEND_ROWS)
        return remote(own.at[block], from_slow.at[block], send_sem.at[1, i], recv_slow_sem.at[i], slow_id)

    def conf_to_fast():
        return remote(conf_out, conf_fast, conf_sem.at[0], conf_sem.at[1], fast_id)

    def conf_to_slow():
        return remote(conf_out, conf_slow, conf_sem.at[2], conf_sem.at[3], slow_id)

    for load in loads[:2]:
        load.wait()
    for load in loads[6:]:
        load.start()
    for begin, end in EMBED_BLOCKS:
        if begin == first_rows:
            loads[2].wait()
        own[begin:end, :] = dot(tokens[begin:end, :], w_embed[...]).astype(BF16)
        if begin == 0:

            @pl.when(chained)
            def _():
                pl.semaphore_wait(barrier, 2)

            @pl.when(jnp.logical_not(chained))
            def _():
                pl.semaphore_wait(barrier, 1)
                from_slow[...] = jnp.zeros_like(from_slow)
                back_slow[...] = jnp.zeros_like(back_slow)
                conf_slow[...] = jnp.zeros_like(conf_slow)

        @pl.when(chained)
        def _(begin=begin, end=end):
            for i in range(begin // SEND_ROWS, end // SEND_ROWS):
                to_slow(i).start()

        for i in range(begin // SEND_ROWS, end // SEND_ROWS):
            to_fast(i).start()

    for load in loads[3:6]:
        load.wait()
    first, second = pair_ref[0, 0], pair_ref[0, 1]
    has_fast = jnp.logical_or(first == fast, second == fast)
    has_slow = jnp.logical_or(first == slow, second == slow)
    u_image = jnp.where(has_fast, fast, me)
    u_first = (first == u_image).astype(F32)
    f_fast, f_slow = has_fast.astype(F32), has_slow.astype(F32)
    conf_first = conf_ref[0, 0:1, :].astype(F32)
    conf_second = conf_ref[0, 1:2, :].astype(F32)
    conf_u = conf_first * u_first + conf_second * (1.0 - u_first)
    conf_w = conf_second * u_first + conf_first * (1.0 - u_first)
    conf_out[...] = jnp.concatenate(
        [
            conf_u * f_fast,
            conf_w * f_slow,
            conf_u * (1.0 - f_fast),
            conf_w * (1.0 - f_slow),
            jnp.zeros((4, tok), F32),
        ],
        axis=0,
    )
    conf_to_fast().start()

    @pl.when(chained)
    def _():
        conf_to_slow().start()


    lower_half = lax.broadcasted_iota(jnp.int32, (1, HEADS * HEAD_DIM), 1) % PAIRED < HEAD_DIM
    half = lax.broadcasted_iota(jnp.int32, (1, PAIRED), 1) < HEAD_DIM

    def put_query(block, x, even_ref, odd_ref):
        q = dot(x, w_query[...]) * (LOG2E / HEAD_DIM**0.5)
        even_ref[block, :] = jnp.where(lower_half, q, 0.0).astype(BF16)
        odd_ref[block, :] = jnp.where(lower_half, 0.0, q).astype(BF16)

    def put_key(block, x, k_ref):
        k_ref[block, :] = dot(x, w_key[...]).astype(BF16)

    def put_value(block, x, v_ref):
        v_ref[block, :] = dot(x, w_value[...]).astype(BF16)

    ones = jnp.ones((tok, PAIRED), BF16)

    def lanes(h):
        return slice(h // 2 * PAIRED, (h // 2 + 1) * PAIRED)

    class Attention:
        def __init__(self, block, x_ref, q_refs, k_ref, v_ref, keys):
            self.block, self.keys = slice(*block), slice(*keys)
            self.ahead = 512 * 512 // ((block[1] - block[0]) * (keys[1] - keys[0]))
            self.x_ref, self.q_refs, self.k_ref, self.v_ref = x_ref, q_refs, k_ref, v_ref
            self.scores = {h: self.scores_of(h) for h in range(self.ahead)}

        def scores_of(self, h):
            return lax.dot_general(
                self.q_refs[h % 2][self.block, lanes(h)],
                self.k_ref[self.keys, lanes(h)],
                (((1,), (1,)), ((), ())),
                preferred_element_type=F32,
            )

        def heads(self):
            for h in range(HEADS):
                if h + self.ahead < HEADS:
                    self.scores[h + self.ahead] = self.scores_of(h + self.ahead)
                s = self.scores.pop(h)
                top = jnp.max(s, axis=1, keepdims=True)
                expo = jnp.exp2(s - top).astype(BF16)
                values = jnp.concatenate([self.v_ref[self.keys, lanes(h)], ones[: s.shape[1]]], axis=1)
                result = dot(expo, values)
                if h % 2 == 0:
                    even = result
                    continue
                total = jnp.where(half, even[:, :PAIRED], result[:, :PAIRED])
                weight = jnp.where(half, even[:, PAIRED:], result[:, PAIRED:])
                context[self.block, lanes(h)] = (total / weight).astype(BF16)

        def normed(self):
            mixed = self.x_ref[self.block, :].astype(F32) + dot(context[self.block, :], w_out[...])
            center = mixed - jnp.mean(mixed, axis=-1, keepdims=True)
            spread = jnp.mean(center * center, axis=-1, keepdims=True)
            return (center * lax.rsqrt(spread + 1e-06) * gain_ref[...][None]).astype(BF16)

    for load in loads[6:10]:
        load.wait()
    for begin, end in TAKE_BLOCKS:
        for i in range(begin // SEND_ROWS, end // SEND_ROWS):
            to_fast(i).wait_recv()
        block = slice(begin, end)
        x = jnp.where(has_fast, from_fast[block, :], own[block, :])
        x_u[block, :] = x
        put_key(block, x, k_u)
        put_value(block, x, v_u)
        put_query(block, x, q_even_u, q_odd_u)

    def back_to_fast(i):
        block = pl.ds(U_BLOCKS[i][0], U_BLOCKS[i][1] - U_BLOCKS[i][0])
        return remote(normed_u.at[block], back_fast.at[block], send_back_sem.at[0, i], recv_back_fast_sem.at[i], fast_id)

    def back_to_slow(i):
        block = pl.ds(W_BLOCKS[i][0], W_BLOCKS[i][1] - W_BLOCKS[i][0])
        return remote(normed_w.at[block], back_slow.at[block], send_back_sem.at[1, i], recv_back_slow_sem.at[i], slow_id)

    def end_w(i, attention):
        normed_w[attention.block, :] = attention.normed()

        @pl.when(chained)
        def _():
            back_to_slow(i).start()

    pending = None
    for i, (begin, end) in enumerate(W_BLOCKS):

        @pl.when(chained)
        def _(begin=begin, end=end):
            for part in range(begin // SEND_ROWS, end // SEND_ROWS):
                to_slow(part).wait_recv()

        block = slice(begin, end)
        x = jnp.where(has_slow, from_slow[block, :], own[block, :])
        x_w[block, :] = x
        put_query(block, x, q_even_w, q_odd_w)
        put_key(block, x, k_w)
        put_value(block, x, v_w)
        if pending is not None:
            end_w(i - 1, pending)
        pending = Attention((begin, end), x_w, (q_even_w, q_odd_w), k_u, v_u, (0, tok))
        pending.heads()

    attentions = []
    for i, block in enumerate(U_BLOCKS):
        attentions.append(
            Attention(block, x_u, (q_even_u, q_odd_u), k_w, v_w, (0, tok))
        )
        if i == 0:
            end_w(len(W_BLOCKS) - 1, pending)
        else:
            normed_u[attentions[i - 1].block, :] = attentions[i - 1].normed()
            back_to_fast(i - 1).start()
        attentions[i].heads()
    normed_u[attentions[-1].block, :] = attentions[-1].normed()
    back_to_fast(len(U_BLOCKS) - 1).start()

    loads[10].wait()
    conf_to_fast().wait()

    @pl.when(chained)
    def _():
        conf_to_slow().wait()

    parts = jnp.concatenate(
        [conf_fast[0:1, :], conf_slow[1:2, :], conf_out[2:4, :], jnp.zeros((4, tok), F32)], axis=0
    )
    weight = jnp.sum(parts, axis=0, keepdims=True)
    shares = jnp.transpose(parts / jnp.maximum(weight, 1.0))

    fast_here, slow_here = 0, 0
    for begin, end in HEAD_BLOCKS + ((HEAD_ROWS, tok),):
        block = slice(begin, end)
        while fast_here < len(U_BLOCKS) and U_BLOCKS[fast_here][0] < end:
            back_to_fast(fast_here).wait_recv()
            fast_here += 1
        behind = slow_here
        while slow_here < len(W_BLOCKS) and W_BLOCKS[slow_here][0] < end:
            slow_here += 1

        @pl.when(chained)
        def _(behind=behind, slow_here=slow_here):
            for i in range(behind, slow_here):
                back_to_slow(i).wait_recv()

        s = shares[block, :]
        merged = s[:, 0:1] * back_fast[block, :].astype(F32)
        merged += s[:, 1:2] * back_slow[block, :].astype(F32)
        merged += s[:, 2:3] * normed_u[block, :].astype(F32)
        merged += s[:, 3:4] * normed_w[block, :].astype(F32)
        merged = merged.astype(BF16)
        if begin < HEAD_ROWS:
            for left in range(0, w_head.shape[1], HEAD_TILE):
                tile = slice(left, min(left + HEAD_TILE, w_head.shape[1]))
                head_ref[block, tile] = dot(merged, w_head[:, tile]).astype(BF16)
        else:
            merged_ref[...] = merged

    for i in range(sends):
        to_fast(i).wait_send()
    for i in range(len(U_BLOCKS)):
        back_to_fast(i).wait_send()

    @pl.when(chained)
    def _():
        for i in range(sends):
            to_slow(i).wait_send()
        for i in range(len(W_BLOCKS)):
            back_to_slow(i).wait_send()


def merged_normed(mesh_shape, pair_list, confidence, tokens, w_embed, w_query, w_key, w_value, w_out, norm_gain, w_head):
    tok = tokens.shape[1]
    width = w_embed.shape[1]
    in_hbm = pl.BlockSpec(memory_space=pl.ANY)
    operands = (pair_list, confidence, norm_gain, tokens, w_embed, w_query, w_key, w_value, w_out, w_head)
    return pl.pallas_call(
        functools.partial(kernel, mesh_shape),
        out_shape=(
            jax.ShapeDtypeStruct((tok - HEAD_ROWS, width), BF16),
            jax.ShapeDtypeStruct((HEAD_ROWS, w_head.shape[1]), BF16),
            jax.ShapeDtypeStruct(w_head.shape, BF16),
        ),
        in_specs=[in_hbm] * len(operands),
        out_specs=[pl.BlockSpec(memory_space=pltpu.VMEM)] * 3,
        scratch_shapes=[
            pltpu.SMEM(pair_list.shape, jnp.int32),
            pltpu.VMEM(confidence.shape, jnp.int32),
            pltpu.VMEM(norm_gain.shape, F32),
            pltpu.VMEM(tokens.shape[1:], BF16),
            pltpu.VMEM(w_embed.shape, BF16),
            pltpu.VMEM(w_query.shape, BF16),
            pltpu.VMEM(w_key.shape, BF16),
            pltpu.VMEM(w_value.shape, BF16),
            pltpu.VMEM(w_out.shape, BF16),
        ]
        + [pltpu.VMEM((tok, width), BF16)] * 18
        + [pltpu.VMEM((8, tok), F32)] * 3
        + [
            pltpu.SemaphoreType.DMA((len(operands) + 1,)),
            pltpu.SemaphoreType.DMA((2, tok // SEND_ROWS)),
            pltpu.SemaphoreType.DMA((tok // SEND_ROWS,)),
            pltpu.SemaphoreType.DMA((tok // SEND_ROWS,)),
            pltpu.SemaphoreType.DMA((2, len(W_BLOCKS))),
            pltpu.SemaphoreType.DMA((len(U_BLOCKS),)),
            pltpu.SemaphoreType.DMA((len(W_BLOCKS),)),
            pltpu.SemaphoreType.DMA((4,)),
        ],
        compiler_params=pltpu.CompilerParams(
            collective_id=0, has_side_effects=True, vmem_limit_bytes=40 * 2**20
        ),
        name="pair_attention",
    )(*(pltpu.with_memory_space_constraint(a, pltpu.HBM) for a in operands))


def finish_kernel(merged_ref, head_ref, w_head, out_ref, last, copy_sem):
    copy = pltpu.make_async_copy(head_ref, out_ref.at[0, 0:HEAD_ROWS], copy_sem.at[0])
    copy.start()
    copies = [copy]
    width = w_head.shape[1]
    for i, left in enumerate(range(0, width, FINISH_TILE)):
        tile = slice(left, min(left + FINISH_TILE, width))
        last[:, tile] = dot(merged_ref[...], w_head[:, tile]).astype(BF16)
        copy = pltpu.make_async_copy(
            last.at[:, tile], out_ref.at[0, HEAD_ROWS : out_ref.shape[1], tile], copy_sem.at[1 + i]
        )
        copy.start()
        copies.append(copy)
    for copy in copies:
        copy.wait()


def finished(merged, head, w_head):
    tok, width = merged.shape[0] + head.shape[0], w_head.shape[1]
    return pl.pallas_call(
        finish_kernel,
        out_shape=jax.ShapeDtypeStruct((1, tok, width), BF16),
        in_specs=[pl.BlockSpec(memory_space=pltpu.VMEM)] * 3,
        out_specs=pl.BlockSpec(memory_space=pltpu.HBM),
        scratch_shapes=[
            pltpu.VMEM((merged.shape[0], width), BF16),
            pltpu.SemaphoreType.DMA((1 + -(-width // FINISH_TILE),)),
        ],
        compiler_params=pltpu.CompilerParams(vmem_limit_bytes=16 * 2**20),
        name="head_of_last_rows",
    )(merged, head, w_head)


def solution(mesh):
    mesh_shape = (mesh.shape["group"], mesh.shape["dev"])

    def on_device(
        tokens, pair_list, confidence, w_embed, w_query, w_key, w_value, w_out, norm_gain, w_head
    ):
        return finished(
            *merged_normed(
                mesh_shape, pair_list, confidence, tokens, w_embed, w_query, w_key, w_value, w_out, norm_gain, w_head
            )
        )

    along = ("group", "dev")
    in_specs = (P(along, None, None), P(along, None), P(along, None, None)) + (P(),) * 7
    return jax.shard_map(
        on_device, mesh=mesh, in_specs=in_specs, out_specs=P(along, None, None), check_vma=False
    )
```

```python
import functools

import jax
import jax.numpy as jnp
from jax import lax
from jax.experimental import pallas as pl
from jax.experimental.pallas import tpu as pltpu
from jax.sharding import PartitionSpec as P

HEADS = 12
HEAD_DIM = 64
PAIRED = 2 * HEAD_DIM
LOG2E = 1.4426950408889634
MESH = pl.DeviceIdType.MESH
BF16 = jnp.bfloat16
F32 = jnp.float32
SEND_ROWS = 128
EMBED_BLOCKS = ((0, 128), (128, 256), (256, 512))
TAKE_BLOCKS = ((0, 256), (256, 512))
W_BLOCKS = ((0, 128), (128, 256), (256, 384), (384, 512))
U_BLOCKS = ((0, 256), (256, 512))
HEAD_BLOCKS = ((0, 256), (256, 384))
HEAD_ROWS = 384
HEAD_TILE = 512
FINISH_TILE = 1152


def dot(a, b):
    return jnp.dot(a, b, preferred_element_type=F32)


def kernel(
    mesh_shape,
    pair_hbm,
    conf_hbm,
    gain_hbm,
    tokens_hbm,
    w_embed_hbm,
    w_query_hbm,
    w_key_hbm,
    w_value_hbm,
    w_out_hbm,
    w_head_hbm,
    merged_ref,
    head_ref,
    w_head,
    pair_ref,
    conf_ref,
    gain_ref,
    tokens,
    w_embed,
    w_query,
    w_key,
    w_value,
    w_out,
    own,
    from_fast,
    from_slow,
    x_u,
    x_w,
    q_even_u,
    q_odd_u,
    q_even_w,
    q_odd_w,
    k_u,
    k_w,
    v_u,
    v_w,
    context,
    normed_u,
    normed_w,
    back_fast,
    back_slow,
    conf_out,
    conf_fast,
    conf_slow,
    load_sem,
    send_sem,
    recv_fast_sem,
    recv_slow_sem,
    send_back_sem,
    recv_back_fast_sem,
    recv_back_slow_sem,
    conf_sem,
):
    n_group, n_dev = mesh_shape
    n = n_group * n_dev
    me = lax.axis_index("group") * n_dev + lax.axis_index("dev")
    odd = lax.rem(me, 2)
    fast = me + 1 - 2 * odd
    slow = lax.rem(me + 2 * odd - 1 + n, n)
    fast_id = (lax.div(fast, n_dev), lax.rem(fast, n_dev))
    slow_id = (lax.div(slow, n_dev), lax.rem(slow, n_dev))
    tok = own.shape[0]
    sends = tok // SEND_ROWS
    chained = jnp.logical_and(slow != 0, me != 0)

    def rows_of(step, size):
        return pl.ds(step * size, size)

    first_rows = EMBED_BLOCKS[0][1]
    loads = [
        pltpu.make_async_copy(src, dst, load_sem.at[i])
        for i, (src, dst) in enumerate(
            (
                (tokens_hbm.at[0, 0:first_rows], tokens.at[0:first_rows]),
                (w_embed_hbm, w_embed),
                (tokens_hbm.at[0, first_rows:tok], tokens.at[first_rows:tok]),
                (pair_hbm, pair_ref),
                (conf_hbm, conf_ref),
                (gain_hbm, gain_ref),
                (w_key_hbm, w_key),
                (w_value_hbm, w_value),
                (w_query_hbm, w_query),
                (w_out_hbm, w_out),
                (w_head_hbm, w_head),
            )
        )
    ]
    for load in loads[:6]:
        load.start()

    barrier = pltpu.get_barrier_semaphore()
    pl.semaphore_signal(barrier, inc=1, device_id=fast_id, device_id_type=MESH)

    @pl.when(chained)
    def _():
        pl.semaphore_signal(barrier, inc=1, device_id=slow_id, device_id_type=MESH)


    def remote(src, dst, send, recv, target):
        return pltpu.make_async_remote_copy(
            src_ref=src,
            dst_ref=dst,
            send_sem=send,
            recv_sem=recv,
            device_id=target,
            device_id_type=MESH,
        )

    def to_fast(i):
        block = rows_of(i, SEND_ROWS)
        return remote(own.at[block], from_fast.at[block], send_sem.at[0, i], recv_fast_sem.at[i], fast_id)

    def to_slow(i):
        block = rows_of(i, SEND_ROWS)
        return remote(own.at[block], from_slow.at[block], send_sem.at[1, i], recv_slow_sem.at[i], slow_id)

    def conf_to_fast():
        return remote(conf_out, conf_fast, conf_sem.at[0], conf_sem.at[1], fast_id)

    def conf_to_slow():
        return remote(conf_out, conf_slow, conf_sem.at[2], conf_sem.at[3], slow_id)

    for load in loads[:2]:
        load.wait()
    for load in loads[6:]:
        load.start()
    for begin, end in EMBED_BLOCKS:
        if begin == first_rows:
            loads[2].wait()
        own[begin:end, :] = dot(tokens[begin:end, :], w_embed[...]).astype(BF16)
        if begin == 0:

            @pl.when(chained)
            def _():
                pl.semaphore_wait(barrier, 2)

            @pl.when(jnp.logical_not(chained))
            def _():
                pl.semaphore_wait(barrier, 1)
                from_slow[...] = jnp.zeros_like(from_slow)
                back_slow[...] = jnp.zeros_like(back_slow)
                conf_slow[...] = jnp.zeros_like(conf_slow)

        @pl.when(chained)
        def _(begin=begin, end=end):
            for i in range(begin // SEND_ROWS, end // SEND_ROWS):
                to_slow(i).start()

        for i in range(begin // SEND_ROWS, end // SEND_ROWS):
            to_fast(i).start()

    for load in loads[3:6]:
        load.wait()
    first, second = pair_ref[0, 0], pair_ref[0, 1]
    has_fast = jnp.logical_or(first == fast, second == fast)
    has_slow = jnp.logical_or(first == slow, second == slow)
    u_image = jnp.where(has_fast, fast, me)
    u_first = (first == u_image).astype(F32)
    f_fast, f_slow = has_fast.astype(F32), has_slow.astype(F32)
    conf_first = conf_ref[0, 0:1, :].astype(F32)
    conf_second = conf_ref[0, 1:2, :].astype(F32)
    conf_u = conf_first * u_first + conf_second * (1.0 - u_first)
    conf_w = conf_second * u_first + conf_first * (1.0 - u_first)
    conf_out[...] = jnp.concatenate(
        [
            conf_u * f_fast,
            conf_w * f_slow,
            conf_u * (1.0 - f_fast),
            conf_w * (1.0 - f_slow),
            jnp.zeros((4, tok), F32),
        ],
        axis=0,
    )
    conf_to_fast().start()

    @pl.when(chained)
    def _():
        conf_to_slow().start()


    lower_half = lax.broadcasted_iota(jnp.int32, (1, HEADS * HEAD_DIM), 1) % PAIRED < HEAD_DIM
    half = lax.broadcasted_iota(jnp.int32, (1, PAIRED), 1) < HEAD_DIM

    def put_query(block, x, even_ref, odd_ref):
        q = dot(x, w_query[...]) * (LOG2E / HEAD_DIM**0.5)
        even_ref[block, :] = jnp.where(lower_half, q, 0.0).astype(BF16)
        odd_ref[block, :] = jnp.where(lower_half, 0.0, q).astype(BF16)

    def put_key(block, x, k_ref):
        k_ref[block, :] = dot(x, w_key[...]).astype(BF16)

    def put_value(block, x, v_ref):
        v_ref[block, :] = dot(x, w_value[...]).astype(BF16)

    ones = jnp.ones((tok, PAIRED), BF16)

    def lanes(h):
        return slice(h // 2 * PAIRED, (h // 2 + 1) * PAIRED)

    class Attention:
        def __init__(self, block, x_ref, q_refs, k_ref, v_ref, keys):
            self.block, self.keys = slice(*block), slice(*keys)
            self.ahead = 512 * 512 // ((block[1] - block[0]) * (keys[1] - keys[0]))
            self.x_ref, self.q_refs, self.k_ref, self.v_ref = x_ref, q_refs, k_ref, v_ref
            self.scores = {h: self.scores_of(h) for h in range(self.ahead)}

        def scores_of(self, h):
            return lax.dot_general(
                self.q_refs[h % 2][self.block, lanes(h)],
                self.k_ref[self.keys, lanes(h)],
                (((1,), (1,)), ((), ())),
                preferred_element_type=F32,
            )

        def heads(self):
            for h in range(HEADS):
                if h + self.ahead < HEADS:
                    self.scores[h + self.ahead] = self.scores_of(h + self.ahead)
                s = self.scores.pop(h)
                top = jnp.max(s, axis=1, keepdims=True)
                expo = jnp.exp2(s - top).astype(BF16)
                values = jnp.concatenate([self.v_ref[self.keys, lanes(h)], ones[: s.shape[1]]], axis=1)
                result = dot(expo, values)
                if h % 2 == 0:
                    even = result
                    continue
                total = jnp.where(half, even[:, :PAIRED], result[:, :PAIRED])
                weight = jnp.where(half, even[:, PAIRED:], result[:, PAIRED:])
                context[self.block, lanes(h)] = (total / weight).astype(BF16)

        def normed(self):
            mixed = self.x_ref[self.block, :].astype(F32) + dot(context[self.block, :], w_out[...])
            center = mixed - jnp.mean(mixed, axis=-1, keepdims=True)
            spread = jnp.mean(center * center, axis=-1, keepdims=True)
            return (center * lax.rsqrt(spread + 1e-06) * gain_ref[...][None]).astype(BF16)

    for load in loads[6:10]:
        load.wait()
    for begin, end in TAKE_BLOCKS:
        for i in range(begin // SEND_ROWS, end // SEND_ROWS):
            to_fast(i).wait_recv()
        block = slice(begin, end)
        x = jnp.where(has_fast, from_fast[block, :], own[block, :])
        x_u[block, :] = x
        put_key(block, x, k_u)
        put_value(block, x, v_u)
        put_query(block, x, q_even_u, q_odd_u)

    def back_to_fast(i):
        block = pl.ds(U_BLOCKS[i][0], U_BLOCKS[i][1] - U_BLOCKS[i][0])
        return remote(normed_u.at[block], back_fast.at[block], send_back_sem.at[0, i], recv_back_fast_sem.at[i], fast_id)

    def back_to_slow(i):
        block = pl.ds(W_BLOCKS[i][0], W_BLOCKS[i][1] - W_BLOCKS[i][0])
        return remote(normed_w.at[block], back_slow.at[block], send_back_sem.at[1, i], recv_back_slow_sem.at[i], slow_id)

    def end_w(i, attention):
        normed_w[attention.block, :] = attention.normed()

        @pl.when(chained)
        def _():
            back_to_slow(i).start()

    for i, (begin, end) in enumerate(W_BLOCKS):

        @pl.when(chained)
        def _(begin=begin, end=end):
            for part in range(begin // SEND_ROWS, end // SEND_ROWS):
                to_slow(part).wait_recv()

        block = slice(begin, end)
        x = jnp.where(has_slow, from_slow[block, :], own[block, :])
        x_w[block, :] = x
        put_query(block, x, q_even_w, q_odd_w)
        put_key(block, x, k_w)
        put_value(block, x, v_w)
        pending = Attention((begin, end), x_w, (q_even_w, q_odd_w), k_u, v_u, (0, tok))
        pending.heads()
        if end < tok:
            end_w(i, pending)

    loads[10].wait()
    conf_to_fast().wait()

    @pl.when(chained)
    def _():
        conf_to_slow().wait()

    parts = jnp.concatenate(
        [conf_fast[0:1, :], conf_slow[1:2, :], conf_out[2:4, :], jnp.zeros((4, tok), F32)], axis=0
    )
    weight = jnp.sum(parts, axis=0, keepdims=True)
    shares = jnp.transpose(parts / jnp.maximum(weight, 1.0))

    attentions = []
    for i, block in enumerate(U_BLOCKS):
        attentions.append(
            Attention(block, x_u, (q_even_u, q_odd_u), k_w, v_w, (0, tok))
        )
        if i == 0:
            end_w(len(W_BLOCKS) - 1, pending)
        else:
            normed_u[attentions[i - 1].block, :] = attentions[i - 1].normed()
            back_to_fast(i - 1).start()
        attentions[i].heads()
    normed_u[attentions[-1].block, :] = attentions[-1].normed()
    back_to_fast(len(U_BLOCKS) - 1).start()

    fast_here, slow_here = 0, 0
    for begin, end in HEAD_BLOCKS + ((HEAD_ROWS, tok),):
        block = slice(begin, end)
        while fast_here < len(U_BLOCKS) and U_BLOCKS[fast_here][0] < end:
            back_to_fast(fast_here).wait_recv()
            fast_here += 1
        behind = slow_here
        while slow_here < len(W_BLOCKS) and W_BLOCKS[slow_here][0] < end:
            slow_here += 1

        @pl.when(chained)
        def _(behind=behind, slow_here=slow_here):
            for i in range(behind, slow_here):
                back_to_slow(i).wait_recv()

        s = shares[block, :]
        merged = s[:, 0:1] * back_fast[block, :].astype(F32)
        merged += s[:, 1:2] * back_slow[block, :].astype(F32)
        merged += s[:, 2:3] * normed_u[block, :].astype(F32)
        merged += s[:, 3:4] * normed_w[block, :].astype(F32)
        merged = merged.astype(BF16)
        if begin < HEAD_ROWS:
            for left in range(0, w_head.shape[1], HEAD_TILE):
                tile = slice(left, min(left + HEAD_TILE, w_head.shape[1]))
                head_ref[block, tile] = dot(merged, w_head[:, tile]).astype(BF16)
        else:
            merged_ref[...] = merged

    for i in range(sends):
        to_fast(i).wait_send()
    for i in range(len(U_BLOCKS)):
        back_to_fast(i).wait_send()

    @pl.when(chained)
    def _():
        for i in range(sends):
            to_slow(i).wait_send()
        for i in range(len(W_BLOCKS)):
            back_to_slow(i).wait_send()


def merged_normed(mesh_shape, pair_list, confidence, tokens, w_embed, w_query, w_key, w_value, w_out, norm_gain, w_head):
    tok = tokens.shape[1]
    width = w_embed.shape[1]
    in_hbm = pl.BlockSpec(memory_space=pl.ANY)
    operands = (pair_list, confidence, norm_gain, tokens, w_embed, w_query, w_key, w_value, w_out, w_head)
    return pl.pallas_call(
        functools.partial(kernel, mesh_shape),
        out_shape=(
            jax.ShapeDtypeStruct((tok - HEAD_ROWS, width), BF16),
            jax.ShapeDtypeStruct((HEAD_ROWS, w_head.shape[1]), BF16),
            jax.ShapeDtypeStruct(w_head.shape, BF16),
        ),
        in_specs=[in_hbm] * len(operands),
        out_specs=[pl.BlockSpec(memory_space=pltpu.VMEM)] * 3,
        scratch_shapes=[
            pltpu.SMEM(pair_list.shape, jnp.int32),
            pltpu.VMEM(confidence.shape, jnp.int32),
            pltpu.VMEM(norm_gain.shape, F32),
            pltpu.VMEM(tokens.shape[1:], BF16),
            pltpu.VMEM(w_embed.shape, BF16),
            pltpu.VMEM(w_query.shape, BF16),
            pltpu.VMEM(w_key.shape, BF16),
            pltpu.VMEM(w_value.shape, BF16),
            pltpu.VMEM(w_out.shape, BF16),
        ]
        + [pltpu.VMEM((tok, width), BF16)] * 18
        + [pltpu.VMEM((8, tok), F32)] * 3
        + [
            pltpu.SemaphoreType.DMA((len(operands) + 1,)),
            pltpu.SemaphoreType.DMA((2, tok // SEND_ROWS)),
            pltpu.SemaphoreType.DMA((tok // SEND_ROWS,)),
            pltpu.SemaphoreType.DMA((tok // SEND_ROWS,)),
            pltpu.SemaphoreType.DMA((2, len(W_BLOCKS))),
            pltpu.SemaphoreType.DMA((len(U_BLOCKS),)),
            pltpu.SemaphoreType.DMA((len(W_BLOCKS),)),
            pltpu.SemaphoreType.DMA((4,)),
        ],
        compiler_params=pltpu.CompilerParams(
            collective_id=0, has_side_effects=True, vmem_limit_bytes=40 * 2**20
        ),
        name="pair_attention",
    )(*(pltpu.with_memory_space_constraint(a, pltpu.HBM) for a in operands))


def finish_kernel(merged_ref, head_ref, w_head, out_ref, last, copy_sem):
    copy = pltpu.make_async_copy(head_ref, out_ref.at[0, 0:HEAD_ROWS], copy_sem.at[0])
    copy.start()
    copies = [copy]
    width = w_head.shape[1]
    for i, left in enumerate(range(0, width, FINISH_TILE)):
        tile = slice(left, min(left + FINISH_TILE, width))
        last[:, tile] = dot(merged_ref[...], w_head[:, tile]).astype(BF16)
        copy = pltpu.make_async_copy(
            last.at[:, tile], out_ref.at[0, HEAD_ROWS : out_ref.shape[1], tile], copy_sem.at[1 + i]
        )
        copy.start()
        copies.append(copy)
    for copy in copies:
        copy.wait()


def finished(merged, head, w_head):
    tok, width = merged.shape[0] + head.shape[0], w_head.shape[1]
    return pl.pallas_call(
        finish_kernel,
        out_shape=jax.ShapeDtypeStruct((1, tok, width), BF16),
        in_specs=[pl.BlockSpec(memory_space=pltpu.VMEM)] * 3,
        out_specs=pl.BlockSpec(memory_space=pltpu.HBM),
        scratch_shapes=[
            pltpu.VMEM((merged.shape[0], width), BF16),
            pltpu.SemaphoreType.DMA((1 + -(-width // FINISH_TILE),)),
        ],
        compiler_params=pltpu.CompilerParams(vmem_limit_bytes=16 * 2**20),
        name="head_of_last_rows",
    )(merged, head, w_head)


def solution(mesh):
    mesh_shape = (mesh.shape["group"], mesh.shape["dev"])

    def on_device(
        tokens, pair_list, confidence, w_embed, w_query, w_key, w_value, w_out, norm_gain, w_head
    ):
        return finished(
            *merged_normed(
                mesh_shape, pair_list, confidence, tokens, w_embed, w_query, w_key, w_value, w_out, norm_gain, w_head
            )
        )

    along = ("group", "dev")
    in_specs = (P(along, None, None), P(along, None), P(along, None, None)) + (P(),) * 7
    return jax.shard_map(
        on_device, mesh=mesh, in_specs=in_specs, out_specs=P(along, None, None), check_vma=False
    )
```
